512 devices in a mesh: kvseq: 64 (over y, z), tp: 8 (over x, core).
Axes of the slice: x: 4, y: 4, z: 16, core: 2. Of those that a mesh axis runs over, the one named last changes fastest.
Arguments:
- queries: bfloat16 [8, 16384], P(None, 'tp'), may hold values from -6 to 6
- incoming_keys: bfloat16 [8, 1024], P(None, 'tp'), may hold values from -6 to 6
- new_values: bfloat16 [8, 1024], P(None, 'tp'), may hold values from -6 to 6
- key_cache: bfloat16 [8, 4096, 8, 128], P(None, 'kvseq', 'tp'), may hold values from -6 to 6
- value_cache: bfloat16 [8, 4096, 8, 128], P(None, 'kvseq', 'tp'), may hold values from -6 to 6
- lengths: int32 [8], replicated, may hold values from 512 to 4096, as said below
- residual: bfloat16 [8, 16384], P(None, ('kvseq', 'tp')), may hold values from -1 to 1
- norm_gain: bfloat16 [16384], replicated, may hold values from 0.5 to 1.5
- o_weight: bfloat16 [8, 2048, 16384], P('tp', 'kvseq'), may hold values from -0.125 to 0.125
- gate_weight: bfloat16 [26624, 16384], P(('kvseq', 'tp')), may hold values from -0.046875 to 0.046875
- up_weight: bfloat16 [26624, 16384], P(('kvseq', 'tp')), may hold values from -0.046875 to 0.046875
Outputs:
- attended: bfloat16 [8, 8, 2048], P(None, 'tp', 'kvseq')
- updated: bfloat16 [8, 16384], P(None, ('kvseq', 'tp'))
- hidden: bfloat16 [8, 26624], P(None, ('kvseq', 'tp'))
The draws below stay inside these ranges and needn't reach their ends.
Inputs may be any that keep to these rules, and one draw needn't show every extreme that they name: `lengths`: every row has at least 512 cached positions, and some row holds all 4096.
All inputs are finite; a program needn't handle non-finite values.
Results may differ from the reference program's by a relative error of at most 0.03.
Values may be sent and summed in bfloat16 or wider, within the bound.
A program may use at most 64 MiB of HBM per device.

```python
import math
import jax
import jax.numpy as jnp
from jax import lax

DECODING_ROWS = 8
S_DEV = 64
D = 16384
HQ = 128
KEY_VALUE_HEADS = 8
HEAD_SIZE = 128
FF = 26624
CTX = 4096
N_KVSEQ = 64
N_TP = 8


def draw_queries(key, part):
    key = jax.random.fold_in(key, 1)
    shape = (DECODING_ROWS, KEY_VALUE_HEADS, HQ // KEY_VALUE_HEADS, HEAD_SIZE)
    base = jnp.clip(1.5 * jax.random.normal(key, shape, jnp.float32), -6.0, 6.0)
    return base.reshape(DECODING_ROWS, HQ * HEAD_SIZE).astype(jnp.bfloat16)


def draw_key_cache(key, part):
    key = jax.random.fold_in(key, 2)
    shape = (DECODING_ROWS, CTX, KEY_VALUE_HEADS, HEAD_SIZE)
    base = jnp.clip(jax.random.normal(key, shape, jnp.float32), -6.0, 6.0)
    return base.astype(jnp.bfloat16)


def draw_residual(key, part):
    key = jax.random.fold_in(key, 3)
    ramp = 1.0 + 2.0 * lax.broadcasted_iota(jnp.float32, (1, D), 1) / (D - 1)
    base = jnp.clip(0.05 * jax.random.normal(key, (DECODING_ROWS, D), jnp.float32), -0.3, 0.3)
    return (base * ramp).astype(jnp.bfloat16)


def draw_lengths(key, part):
    key = jax.random.fold_in(key, 4)
    first, second = jax.random.split(key)
    spans = jax.random.randint(first, (DECODING_ROWS,), CTX // 8, CTX + 1)
    chosen = jax.random.randint(second, (), 0, DECODING_ROWS)
    return jnp.where(jnp.arange(DECODING_ROWS) == chosen, CTX, spans).astype(jnp.int32)


def strengthened(values, own_key, source, target, parts, factor):
    def block_of(axis_at):
        return (jnp.arange(values.shape[axis_at]) // (values.shape[axis_at] // parts)).reshape((-1,) + (1,) * (values.ndim - 1 - axis_at))

    near = jax.random.permutation(own_key, parts)[block_of(target)]
    far = (block_of(target) + parts // 2) % parts
    return jnp.where((block_of(source) == near) | (block_of(source) == far), factor * values, values)


def levels(own_key, shape, cuts, smallest, high):
    gain, own = 1.0, jax.random.fold_in(own_key, 6)
    for axis_at, blocks in cuts:
        heights = jnp.exp(jax.random.uniform(jax.random.fold_in(own, axis_at), (blocks,), jnp.float32, smallest / len(cuts), high / len(cuts)))
        gain = gain * jnp.repeat(heights, shape[axis_at] // blocks).reshape([-1 if axis == axis_at else 1 for axis in range(len(shape))])
    return gain


def centred(key, dims, deviation, reach, pieces=(), kind=jnp.bfloat16):
    factor_of = levels(key, dims, pieces, -0.22, 0.18) if pieces else 1.0
    drawn = jax.random.normal(key, dims, jnp.float32) * deviation * factor_of
    return jnp.minimum(jnp.maximum(drawn, -reach), reach).astype(kind)


def gaussian_with(key, shape, width, most, cuts, heavy, kind=jnp.bfloat16):
    result = width * jax.random.normal(key, shape, jnp.float32)
    if cuts:
        result = result * levels(key, shape, cuts, -0.22, 0.18)
    return jnp.clip(strengthened(result, jax.random.fold_in(key, 3), *heavy), -most, most).astype(kind)


def setup_inputs(seed: int = 0) -> dict:
    splits = jax.random.split(jax.random.key(seed), 12)
    queries = draw_queries(jax.random.fold_in(splits[11], 71), 0)
    incoming_keys = centred(splits[1], (DECODING_ROWS, KEY_VALUE_HEADS * HEAD_SIZE), 1.0, 6.0, ((1, 8),))
    new_values = centred(splits[2], (DECODING_ROWS, KEY_VALUE_HEADS * HEAD_SIZE), 1.0, 6.0, ((1, 8),))
    key_cache = draw_key_cache(jax.random.fold_in(splits[11], 71), 0)
    value_cache = centred(splits[4], (DECODING_ROWS, CTX, KEY_VALUE_HEADS, HEAD_SIZE), 1.0, 6.0, ((1, 64), (2, 8)))
    lengths = draw_lengths(jax.random.fold_in(splits[11], 71), 0)
    residual = draw_residual(jax.random.fold_in(splits[11], 71), 0)
    norm_gain = jnp.clip(1.0 + 0.1 * jax.random.normal(splits[7], (D,), jnp.float32), 0.5, 1.5).astype(jnp.bfloat16)
    o_weight = gaussian_with(splits[8], (N_TP, HQ * HEAD_SIZE // N_TP, D), (HQ * HEAD_SIZE) ** -0.5, 0.125, ((0, 8), (1, 64)), (1, 2, 64, 4.0))
    gate_weight = centred(splits[9], (FF, D), D ** -0.5, 0.046875, ((0, 512),))
    up_weight = centred(splits[10], (FF, D), D ** -0.5, 0.046875, ((0, 512),))
    return dict(queries=queries, incoming_keys=incoming_keys, new_values=new_values, key_cache=key_cache, value_cache=value_cache, lengths=lengths, residual=residual, norm_gain=norm_gain, o_weight=o_weight, gate_weight=gate_weight, up_weight=up_weight)


norm_eps = 1e-05

def reference(queries, incoming_keys, new_values, key_cache, value_cache, lengths, residual, norm_gain, o_weight, gate_weight, up_weight):
    blocks = N_KVSEQ
    group = HQ // KEY_VALUE_HEADS
    score_scale = 1.0 / math.sqrt(HEAD_SIZE)
    query_head_count = queries.astype(jnp.float32).reshape(DECODING_ROWS, KEY_VALUE_HEADS, group, HEAD_SIZE)
    keys = key_cache.astype(jnp.float32).reshape(DECODING_ROWS, blocks, S_DEV, KEY_VALUE_HEADS, HEAD_SIZE)
    values = value_cache.astype(jnp.float32).reshape(DECODING_ROWS, blocks, S_DEV, KEY_VALUE_HEADS, HEAD_SIZE)
    scores = jnp.einsum('bkgd,bnskd->bnkgs', query_head_count, keys) * score_scale
    posit = (jnp.arange(blocks, dtype=jnp.int32)[:, None] * S_DEV + jnp.arange(S_DEV, dtype=jnp.int32)[None, :]).astype(jnp.int32)
    live = posit[None, :, None, None, :] < lengths[:, None, None, None, None]
    incoming_token = jnp.einsum('cuxt,cut->cux', query_head_count, incoming_keys.astype(jnp.float32).reshape(DECODING_ROWS, KEY_VALUE_HEADS, HEAD_SIZE)) * score_scale
    first = (jnp.arange(blocks) == 0)[None, :, None, None]
    top = lax.optimization_barrier(jnp.max(jnp.where(live, scores, -10000.0), axis=-1))
    top = jnp.where(first, jnp.maximum(top, incoming_token[:, None]), top)
    probs = jnp.where(live, jnp.exp(scores - top[..., None]), 0.0)
    pnew = jnp.where(first, jnp.exp(incoming_token[:, None] - top), 0.0)
    total = lax.optimization_barrier(jnp.sum(probs, axis=-1)) + pnew
    probs_low = lax.optimization_barrier(probs.astype(jnp.bfloat16)).astype(jnp.float32)
    pnew_low = lax.optimization_barrier(pnew.astype(jnp.bfloat16)).astype(jnp.float32)
    numer = jnp.einsum('bnkgs,bnskd->bnkgd', probs_low, values)
    numer = numer + pnew_low[..., None] * new_values.astype(jnp.float32).reshape(DECODING_ROWS, 1, KEY_VALUE_HEADS, 1, HEAD_SIZE)
    floor = jnp.maximum(total, 1.0)
    partial_value = (numer / floor[..., None]).astype(jnp.bfloat16)
    lse = top + jnp.log(floor)
    peak = lax.optimization_barrier(jnp.max(lse, axis=1, keepdims=True))
    share = jnp.exp(lse - peak)
    attended = (lax.optimization_barrier(jnp.sum(share[..., None] * partial_value.astype(jnp.float32), axis=1)) / lax.optimization_barrier(jnp.sum(share, axis=1))[..., None]).astype(jnp.bfloat16)
    flat = attended.reshape(DECODING_ROWS, HQ * HEAD_SIZE)
    h = jnp.dot(flat, o_weight.reshape(HQ * HEAD_SIZE, D), preferred_element_type=jnp.float32) + residual.astype(jnp.float32)
    updated = h.astype(jnp.bfloat16)
    inverse = lax.rsqrt(lax.optimization_barrier(jnp.mean(h * h, axis=-1, keepdims=True)) + norm_eps)
    normed = (h * inverse * norm_gain.astype(jnp.float32)[None, :]).astype(jnp.bfloat16)
    gate = jnp.dot(normed, gate_weight.T, preferred_element_type=jnp.float32)
    up = jnp.dot(normed, up_weight.T, preferred_element_type=jnp.float32)
    hidden = (jax.nn.silu(gate) * up).astype(jnp.bfloat16)
    return (attended.reshape(DECODING_ROWS, N_TP, HQ * HEAD_SIZE // N_TP), updated, hidden)
```

```python
import math

import jax
import jax.numpy as jnp
from jax import lax
from jax.experimental import pallas as pl
from jax.experimental.pallas import tpu as pltpu
from jax.sharding import PartitionSpec as P

norm_eps = 1e-05
MESH = pl.DeviceIdType.MESH
F32, BF16 = jnp.float32, jnp.bfloat16
UNROLL = True


def place():
    kv, tp = lax.axis_index("kvseq"), lax.axis_index("tp")
    return kv // 16, kv % 16, tp // 2, tp % 2


def z_peer(k):
    y, z, x, c = place()
    step = jnp.where(k % 2 == 0, 8 + k // 2, 8 - (k + 1) // 2)
    return (y * 16 + (z + step) % 16, x * 2 + c)


def far_first(a):
    return jnp.where(a == 0, 2, jnp.where(a == 1, 1, jnp.where(a == 2, 3, 0)))


def plane_peer(k):
    y, z, x, c = place()
    py = (y + far_first(k // 8)) % 4
    px = (x + far_first((k // 2) % 4)) % 4
    return py, px, (c + 1 - k % 2) % 2


def loop(n, body):
    def step(k, carry):
        body(k)
        return carry

    lax.fori_loop(0, n, step, 0, unroll=UNROLL)


def kernel(
    lengths_ref,
    q_hbm,
    ik_hbm,
    nv_hbm,
    k_hbm,
    v_hbm,
    res_hbm,
    gain_hbm,
    ow_hbm,
    gate_hbm,
    up_hbm,
    att_out,
    upd_out,
    hid_out,
    q_ref,
    ik_ref,
    nv_ref,
    k_ref,
    v_ref,
    res_ref,
    gain_ref,
    ow,
    gate_w,
    up_w,
    gain32,
    s1,
    z1,
    rsrc,
    rbuf,
    psrc,
    pbuf,
    wbuf,
    z2src,
    z2,
    hsrc,
    hbuf,
    hg,
    local_sems,
    send_sems,
    recv_sems,
):
    y, z, x, c = place()
    t = x * 2 + c
    j = y * 16 + z
    slot_ty = t * 4 + y
    slot_m = y * 8 + t
    barrier = pltpu.get_barrier_semaphore()

    def greet_z(k):
        pl.semaphore_signal(barrier, inc=1, device_id=z_peer(k), device_id_type=MESH)

    def greet_plane(k):
        py, px, pc = plane_peer(k)
        pl.semaphore_signal(
            barrier, inc=1, device_id=(py * 16 + z, px * 2 + pc), device_id_type=MESH
        )

    loop(15, greet_z)
    loop(31, greet_plane)

    small = []
    for i, (src, dst) in enumerate(
        (
            (q_hbm, q_ref),
            (k_hbm, k_ref),
            (ik_hbm, ik_ref),
            (v_hbm, v_ref),
            (nv_hbm, nv_ref),
            (res_hbm, res_ref),
            (gain_hbm, gain_ref),
        )
    ):
        small.append(pltpu.make_async_copy(src, dst, local_sems.at[4 + i]))
        small[-1].start()
    ow_load = pltpu.make_async_copy(ow_hbm, ow, local_sems.at[0])
    gate_load = pltpu.make_async_copy(gate_hbm, gate_w, local_sems.at[1])
    up_load = pltpu.make_async_copy(up_hbm, up_w, local_sems.at[2])
    ow_load.start()
    gate_load.start()
    up_load.start()

    for i in range(5):
        small[i].wait()

    scale = 1.0 / math.sqrt(128)
    qs = [q_ref[:, 128 * h : 128 * h + 128].astype(F32) for h in range(16)]
    q_all = jnp.concatenate(qs, axis=0).astype(BF16)
    contract = (((1,), (1,)), ((), ()))
    s_all = lax.dot_general(q_all, k_ref[...], contract, preferred_element_type=F32) * scale
    row = lax.broadcasted_iota(jnp.int32, (8, 512), 0)
    lane = lax.broadcasted_iota(jnp.int32, (8, 512), 1)
    length = jnp.zeros((8, 512), jnp.int32)
    for b in range(8):
        length = jnp.where(row == b, lengths_ref[b], length)
    live = jnp.logical_and(lane // 64 == row, j * 64 + lane % 64 < length)
    ik = ik_ref[...].astype(F32)
    nv = nv_ref[...].astype(F32)
    first = j == 0
    probs, extra, floors, lses = [], [], [], []
    for h in range(16):
        s = s_all[8 * h : 8 * h + 8]
        fresh = jnp.sum(qs[h] * ik, axis=1, keepdims=True) * scale
        fresh = jnp.where(first, fresh, -1e30)
        top = jnp.max(jnp.where(live, s, -10000.0), axis=1, keepdims=True)
        top = jnp.maximum(top, fresh)
        p = jnp.where(live, jnp.exp(s - top), 0.0)
        pnew = jnp.exp(fresh - top)
        floor = jnp.maximum(jnp.sum(p, axis=1, keepdims=True) + pnew, 1.0)
        probs.append(p)
        extra.append(pnew.astype(BF16).astype(F32) * nv)
        floors.append(floor)
        lses.append(top + jnp.log(floor))
    p_all = jnp.concatenate(probs, axis=0).astype(BF16)
    numer = jnp.dot(p_all, v_ref[...], preferred_element_type=F32)
    part = [(numer[8 * h : 8 * h + 8] + extra[h]) / floors[h] for h in range(16)]

    block = lax.broadcasted_iota(jnp.int32, (8, 128), 1) // 32
    for zq in range(4):
        lse_tile = jnp.zeros((8, 128), F32)
        for yy in range(4):
            lse_tile = jnp.where(block == yy, lses[4 * yy + zq], lse_tile)
        for qq in range(4):
            tile = jnp.zeros((8, 128), F32)
            for yy in range(4):
                moved = part[4 * yy + zq]
                shift = (32 * (yy - qq)) % 128
                if shift:
                    moved = pltpu.roll(moved, shift, 1)
                tile = jnp.where(block == yy, moved, tile)
            s1[4 * zq + qq, 0:8, :] = tile
            s1[4 * zq + qq, 8:16, :] = lse_tile

    small[5].wait()
    small[6].wait()
    spot = lax.broadcasted_iota(jnp.int32, (32, 128), 1)
    want = lax.broadcasted_iota(jnp.int32, (32, 128), 0) + 32 * (t % 4)
    onehot = jnp.where(spot == want, 1.0, 0.0).astype(BF16)
    rtile = jnp.dot(res_ref[...], onehot, preferred_element_type=F32)
    rsrc[...] = rtile
    rbuf[t] = rtile
    gain32[...] = gain_ref[...].astype(F32)
    z1[z] = s1[z]

    pl.semaphore_wait(barrier, 46)

    def send_z1(k):
        kv, tp = z_peer(k)
        pltpu.make_async_remote_copy(
            src_ref=s1.at[kv % 16],
            dst_ref=z1.at[z],
            send_sem=send_sems.at[0],
            recv_sem=recv_sems.at[0],
            device_id=(kv, tp),
            device_id_type=MESH,
        ).start()

    loop(15, send_z1)

    ow_load.wait()

    def send_w(k):
        py, px, pc = plane_peer(k)
        column = pl.multiple_of(512 * (py * 8 + px * 2 + pc), 512)
        pltpu.make_async_remote_copy(
            src_ref=ow.at[:, pl.ds(column, 512)],
            dst_ref=wbuf.at[slot_ty],
            send_sem=send_sems.at[1],
            recv_sem=recv_sems.at[1],
            device_id=(py * 16 + z, px * 2 + pc),
            device_id_type=MESH,
        ).start()

    loop(31, send_w)
    own_column = pl.multiple_of(512 * slot_m, 512)
    own_w = pltpu.make_async_copy(
        ow.at[:, pl.ds(own_column, 512)], wbuf.at[slot_ty], local_sems.at[3]
    )
    own_w.start()

    def send_res(k):
        pltpu.make_async_remote_copy(
            src_ref=rsrc,
            dst_ref=rbuf.at[t],
            send_sem=send_sems.at[2],
            recv_sem=recv_sems.at[2],
            device_id=(j, (t + 1 + k) % 8),
            device_id_type=MESH,
        ).start()

    loop(7, send_res)

    def wait(ref, sem):
        pltpu.make_async_copy(ref, ref, sem).wait()

    wait(z1.at[pl.ds(0, 15)], recv_sems.at[0])
    tops = [z1[i, 8:16, :] for i in range(16)]
    peak = tops[0]
    for i in range(1, 16):
        peak = jnp.maximum(peak, tops[i])
    num = jnp.zeros((8, 128), F32)
    den = jnp.zeros((8, 128), F32)
    for i in range(16):
        w = jnp.exp(tops[i] - peak)
        num = num + w * z1[i, 0:8, :]
        den = den + w
    num = num / den
    den = peak + jnp.log(den)
    psrc[0:8, :] = num
    psrc[8:16, :] = den
    pbuf[slot_ty, 0:8, :] = num
    pbuf[slot_ty, 8:16, :] = den

    def send_p(k):
        py, px, pc = plane_peer(k)
        pltpu.make_async_remote_copy(
            src_ref=psrc,
            dst_ref=pbuf.at[slot_ty],
            send_sem=send_sems.at[3],
            recv_sem=recv_sems.at[3],
            device_id=(py * 16 + z, px * 2 + pc),
            device_id_type=MESH,
        ).start()

    loop(31, send_p)
    wait(pbuf.at[pl.ds(0, 31)], recv_sems.at[3])
    atts = []
    for tt in range(8):
        tops = [pbuf[4 * tt + i, 8:16, :] for i in range(4)]
        peak = jnp.maximum(jnp.maximum(tops[0], tops[1]), jnp.maximum(tops[2], tops[3]))
        num = jnp.zeros((8, 128), F32)
        den = jnp.zeros((8, 128), F32)
        for i in range(4):
            w = jnp.exp(tops[i] - peak)
            num = num + w * pbuf[4 * tt + i, 0:8, :]
            den = den + w
        atts.append(num / den)
    att = jnp.concatenate(atts, axis=1).astype(BF16)

    wait(wbuf.at[pl.ds(0, 31)], recv_sems.at[1])
    own_w.wait()
    h_part = jnp.dot(att, wbuf[...].reshape(1024, 512), preferred_element_type=F32)
    wait(rbuf.at[pl.ds(0, 7)], recv_sems.at[2])
    here = z // 2 == t
    r_low = jnp.where(here, rbuf[0] + rbuf[1] + rbuf[2] + rbuf[3], 0.0)
    r_high = jnp.where(here, rbuf[4] + rbuf[5] + rbuf[6] + rbuf[7], 0.0)
    r_both = jnp.concatenate([r_low, r_high], axis=1)
    h_even = h_part[:, 0:256] + jnp.where(z % 2 == 0, r_both, 0.0)
    h_odd = h_part[:, 256:512] + jnp.where(z % 2 == 1, r_both, 0.0)
    h_low = jnp.concatenate([h_even, h_odd], axis=0).astype(BF16)
    z2src[...] = h_low
    z2[z] = h_low

    def send_z2(k):
        kv, tp = z_peer(k)
        pltpu.make_async_remote_copy(
            src_ref=z2src,
            dst_ref=z2.at[z],
            send_sem=send_sems.at[4],
            recv_sem=recv_sems.at[4],
            device_id=(kv, tp),
            device_id_type=MESH,
        ).start()

    loop(15, send_z2)

    lane128 = lax.broadcasted_iota(jnp.int32, (128, 32), 0)
    col32 = lax.broadcasted_iota(jnp.int32, (128, 32), 1)
    mine = jnp.zeros((8, 128), F32)
    for tt in range(8):
        mine = jnp.where(t == tt, atts[tt], mine)
    pick = jnp.where(lane128 == col32 + 32 * y, 1.0, 0.0).astype(BF16)
    att_out[...] = jnp.dot(mine.astype(BF16), pick, preferred_element_type=F32).astype(BF16)

    wait(z2.at[pl.ds(0, 15)], recv_sems.at[4])
    h_sum = jnp.zeros((16, 256), F32)
    for i in range(16):
        h_sum = h_sum + z2[i].astype(F32)
    h_low = h_sum.astype(BF16)
    hsrc[...] = h_low
    hbuf[slot_m] = h_low

    def send_h(k):
        py, px, pc = plane_peer(k)
        pltpu.make_async_remote_copy(
            src_ref=hsrc,
            dst_ref=hbuf.at[slot_m],
            send_sem=send_sems.at[5],
            recv_sem=recv_sems.at[5],
            device_id=(py * 16 + z, px * 2 + pc),
            device_id_type=MESH,
        ).start()

    loop(31, send_h)
    gate_load.wait()
    up_load.wait()
    wait(hbuf.at[pl.ds(0, 31)], recv_sems.at[5])

    squares = jnp.zeros((8, 128), F32)
    gate = jnp.zeros((8, 52), F32)
    up = jnp.zeros((8, 52), F32)
    for m in range(32):
        full = hbuf[m].astype(F32)
        tiles = []
        for i in range(4):
            r, l = 8 * (i // 2), 128 * (i % 2)
            tile = full[r : r + 8, l : l + 128]
            squares = squares + tile * tile
            tiles.append(tile * gain32[4 * m + i : 4 * m + i + 1, :])
        hg[:, 512 * m : 512 * m + 512] = jnp.concatenate(tiles, axis=1).astype(BF16)
    for m in range(8):
        part_h = hg[:, 2048 * m : 2048 * m + 2048]
        gate = gate + lax.dot_general(
            part_h, gate_w[:, 2048 * m : 2048 * m + 2048], contract, preferred_element_type=F32
        )
        up = up + lax.dot_general(
            part_h, up_w[:, 2048 * m : 2048 * m + 2048], contract, preferred_element_type=F32
        )
    mean = jnp.sum(squares, axis=1, keepdims=True) * (1.0 / 16384)
    inverse = lax.rsqrt(mean + norm_eps)
    gate = gate * inverse
    up = up * inverse
    hid_out[...] = (gate / (1.0 + jnp.exp(-gate)) * up).astype(BF16)

    source = hbuf[y * 8 + z // 2].astype(F32)
    half = jnp.where(z % 2 == 0, source[0:8], source[8:16])
    tile = jnp.where(t // 4 == 0, half[:, 0:128], half[:, 128:256])
    pick = jnp.where(lane128 == col32 + 32 * (t % 4), 1.0, 0.0).astype(BF16)
    upd_out[...] = jnp.dot(tile.astype(BF16), pick, preferred_element_type=F32).astype(BF16)

    wait(s1.at[pl.ds(0, 15)], send_sems.at[0])
    wait(wbuf.at[pl.ds(0, 31)], send_sems.at[1])
    wait(rbuf.at[pl.ds(0, 7)], send_sems.at[2])
    wait(pbuf.at[pl.ds(0, 31)], send_sems.at[3])
    wait(z2.at[pl.ds(0, 15)], send_sems.at[4])
    wait(hbuf.at[pl.ds(0, 31)], send_sems.at[5])


def body(
    queries,
    incoming_keys,
    new_values,
    key_cache,
    value_cache,
    lengths,
    residual,
    norm_gain,
    o_weight,
    gate_weight,
    up_weight,
):
    vmem = pl.BlockSpec(memory_space=pltpu.VMEM)
    hbm = pl.BlockSpec(memory_space=pltpu.HBM)
    attended, updated, hidden = pl.pallas_call(
        kernel,
        out_shape=(
            jax.ShapeDtypeStruct((8, 32), BF16),
            jax.ShapeDtypeStruct((8, 32), BF16),
            jax.ShapeDtypeStruct((8, 52), BF16),
        ),
        in_specs=[pl.BlockSpec(memory_space=pltpu.SMEM)] + [hbm] * 10,
        out_specs=(vmem, vmem, vmem),
        scratch_shapes=[
            pltpu.VMEM((8, 2048), BF16),
            pltpu.VMEM((8, 128), BF16),
            pltpu.VMEM((8, 128), BF16),
            pltpu.VMEM((512, 128), BF16),
            pltpu.VMEM((512, 128), BF16),
            pltpu.VMEM((8, 32), BF16),
            pltpu.VMEM((128, 128), BF16),
            pltpu.VMEM((32, 16384), BF16),
            pltpu.VMEM((52, 16384), BF16),
            pltpu.VMEM((52, 16384), BF16),
            pltpu.VMEM((128, 128), F32),
            pltpu.VMEM((16, 16, 128), F32),
            pltpu.VMEM((16, 16, 128), F32),
            pltpu.VMEM((8, 128), F32),
            pltpu.VMEM((8, 8, 128), F32),
            pltpu.VMEM((16, 128), F32),
            pltpu.VMEM((32, 16, 128), F32),
            pltpu.VMEM((32, 32, 512), BF16),
            pltpu.VMEM((16, 256), BF16),
            pltpu.VMEM((16, 16, 256), BF16),
            pltpu.VMEM((16, 256), BF16),
            pltpu.VMEM((32, 16, 256), BF16),
            pltpu.VMEM((8, 16384), BF16),
            pltpu.SemaphoreType.DMA((11,)),
            pltpu.SemaphoreType.DMA((6,)),
            pltpu.SemaphoreType.DMA((6,)),
        ],
        compiler_params=pltpu.CompilerParams(
            collective_id=0, has_side_effects=True, vmem_limit_bytes=63 * 1024 * 1024
        ),
        name="decode_layer",
    )(
        lengths,
        queries,
        incoming_keys,
        new_values,
        key_cache.reshape(512, 128),
        value_cache.reshape(512, 128),
        residual,
        norm_gain.reshape(128, 128),
        o_weight.reshape(32, 16384),
        gate_weight,
        up_weight,
    )
    return attended.reshape(8, 1, 32), updated, hidden


def solution(mesh):
    in_specs = (
        P(None, "tp"),
        P(None, "tp"),
        P(None, "tp"),
        P(None, "kvseq", "tp", None),
        P(None, "kvseq", "tp", None),
        P(),
        P(None, ("kvseq", "tp")),
        P(),
        P("tp", "kvseq", None),
        P(("kvseq", "tp"), None),
        P(("kvseq", "tp"), None),
    )
    out_specs = (P(None, "tp", "kvseq"), P(None, ("kvseq", "tp")), P(None, ("kvseq", "tp")))
    return jax.shard_map(body, mesh=mesh, in_specs=in_specs, out_specs=out_specs, check_vma=False)
```

```python
import math

import jax
import jax.numpy as jnp
from jax import lax
from jax.experimental import pallas as pl
from jax.experimental.pallas import tpu as pltpu
from jax.sharding import PartitionSpec as P

norm_eps = 1e-05
MESH = pl.DeviceIdType.MESH
F32, BF16 = jnp.float32, jnp.bfloat16
UNROLL = True
W_FIRST, W_SECOND = 12, 22


def place():
    kv, tp = lax.axis_index("kvseq"), lax.axis_index("tp")
    return kv // 16, kv % 16, tp // 2, tp % 2


def z_peer(k):
    y, z, x, c = place()
    step = jnp.where(k % 2 == 0, 8 + k // 2, 8 - (k + 1) // 2)
    return (y * 16 + (z + step) % 16, x * 2 + c)


def z_near(k):
    y, z, x, c = place()
    step = jnp.where(k < 4, 4 - k, k + 8)
    return (y * 16 + (z + step) % 16, x * 2 + c)


def far_first(a):
    return jnp.where(a == 0, 2, jnp.where(a == 1, 1, jnp.where(a == 2, 3, 0)))


def plane_peer(k):
    y, z, x, c = place()
    py = (y + far_first(k // 8)) % 4
    px = (x + far_first((k // 2) % 4)) % 4
    return py, px, (c + 1 - k % 2) % 2


def loop(n, body, start=0):
    def step(k, carry):
        body(k)
        return carry

    lax.fori_loop(start, n, step, 0, unroll=UNROLL)


def merge(nums, tops):
    peak = tops[0]
    for top in tops[1:]:
        peak = jnp.maximum(peak, top)
    num, den = 0.0, 0.0
    for part, top in zip(nums, tops):
        w = jnp.exp(top - peak)
        num = num + w * part
        den = den + w
    return num / den, peak + jnp.log(den)


def encode(num, top):
    spot = lax.broadcasted_iota(jnp.int32, (8, 128), 1) % 32
    high = top.astype(BF16).astype(F32)
    middle = (top - high).astype(BF16).astype(F32)
    low = top - high - middle
    terms = jnp.where(spot == 0, high, jnp.where(spot == 1, middle, jnp.where(spot == 2, low, 0.0)))
    return jnp.concatenate([num, terms], axis=0).astype(BF16)


def decode(tiles):
    n = tiles.shape[0]
    a = lax.broadcasted_iota(jnp.int32, (128, 128), 0) // 32
    b = lax.broadcasted_iota(jnp.int32, (128, 128), 1) // 32
    ones = jnp.where(a == b, 1.0, 0.0).astype(BF16)
    sums = jnp.dot(tiles.reshape(16 * n, 128), ones, preferred_element_type=F32)
    values = tiles.astype(F32)
    return [values[i, 0:8] for i in range(n)], [sums[16 * i + 8 : 16 * i + 16] for i in range(n)]


def kernel(
    lengths_ref,
    q_hbm,
    ik_hbm,
    nv_hbm,
    k_hbm,
    v_hbm,
    res_hbm,
    gain_hbm,
    ow_hbm,
    gate_hbm,
    up_hbm,
    att_out,
    upd_out,
    hid_out,
    q_ref,
    ik_ref,
    nv_ref,
    k_ref,
    v_ref,
    res_ref,
    gain_ref,
    ow,
    gate_w,
    up_w,
    gain32,
    s1,
    zd,
    zp,
    zm,
    zrel,
    zfin,
    rsrc,
    rbuf,
    psrc,
    pbuf,
    wbuf,
    z2src,
    z2,
    hsrc,
    hbuf,
    att_v,
    upd_v,
    hid_v,
    local_sems,
    send_sems,
    recv_sems,
    h_sems,
):
    y, z, x, c = place()
    t = x * 2 + c
    j = y * 16 + z
    slot_ty = t * 4 + y
    slot_m = y * 8 + t
    barrier = pltpu.get_barrier_semaphore()

    def greet_z(k):
        pl.semaphore_signal(barrier, inc=1, device_id=z_near(k), device_id_type=MESH)

    def greet_plane(k):
        py, px, pc = plane_peer(k)
        pl.semaphore_signal(
            barrier, inc=1, device_id=(py * 16 + z, px * 2 + pc), device_id_type=MESH
        )

    loop(8, greet_z)
    loop(31, greet_plane)

    small = []
    for i, (src, dst) in enumerate(
        (
            (q_hbm, q_ref),
            (k_hbm, k_ref),
            (ik_hbm, ik_ref),
            (v_hbm, v_ref),
            (nv_hbm, nv_ref),
            (res_hbm, res_ref),
            (gain_hbm, gain_ref),
        )
    ):
        small.append(pltpu.make_async_copy(src, dst, local_sems.at[4 + i]))
        small[-1].start()
    ow_load = pltpu.make_async_copy(ow_hbm, ow, local_sems.at[0])
    gate_load = pltpu.make_async_copy(gate_hbm, gate_w, local_sems.at[1])
    up_load = pltpu.make_async_copy(up_hbm, up_w, local_sems.at[2])
    ow_load.start()
    gate_load.start()
    up_load.start()

    for i in range(5):
        small[i].wait()

    scale = 1.0 / math.sqrt(128)
    qs = [q_ref[:, 128 * h : 128 * h + 128].astype(F32) for h in range(16)]
    q_all = jnp.concatenate(qs, axis=0).astype(BF16)
    contract = (((1,), (1,)), ((), ()))
    s_all = lax.dot_general(q_all, k_ref[...], contract, preferred_element_type=F32) * scale
    row = lax.broadcasted_iota(jnp.int32, (8, 512), 0)
    lane = lax.broadcasted_iota(jnp.int32, (8, 512), 1)
    length = jnp.zeros((8, 512), jnp.int32)
    for b in range(8):
        length = jnp.where(row == b, lengths_ref[b], length)
    live = jnp.logical_and(lane // 64 == row, j * 64 + lane % 64 < length)
    ik = ik_ref[...].astype(F32)
    nv = nv_ref[...].astype(F32)
    first = j == 0
    probs, extra, floors, lses = [], [], [], []
    for h in range(16):
        s = s_all[8 * h : 8 * h + 8]
        fresh = jnp.sum(qs[h] * ik, axis=1, keepdims=True) * scale
        fresh = jnp.where(first, fresh, -1e30)
        top = jnp.max(jnp.where(live, s, -10000.0), axis=1, keepdims=True)
        top = jnp.maximum(top, fresh)
        p = jnp.where(live, jnp.exp(s - top), 0.0)
        pnew = jnp.exp(fresh - top)
        floor = jnp.maximum(jnp.sum(p, axis=1, keepdims=True) + pnew, 1.0)
        probs.append(p)
        extra.append(pnew.astype(BF16).astype(F32) * nv)
        floors.append(floor)
        lses.append(top + jnp.log(floor))
    p_all = jnp.concatenate(probs, axis=0).astype(BF16)
    numer = jnp.dot(p_all, v_ref[...], preferred_element_type=F32)
    part = [(numer[8 * h : 8 * h + 8] + extra[h]) / floors[h] for h in range(16)]

    block = lax.broadcasted_iota(jnp.int32, (8, 128), 1) // 32
    for zq in range(4):
        lse_tile = jnp.zeros((8, 128), F32)
        for yy in range(4):
            lse_tile = jnp.where(block == yy, lses[4 * yy + zq], lse_tile)
        for qq in range(4):
            tile = jnp.zeros((8, 128), F32)
            for yy in range(4):
                moved = part[4 * yy + zq]
                shift = (32 * (yy - qq)) % 128
                if shift:
                    moved = pltpu.roll(moved, shift, 1)
                tile = jnp.where(block == yy, moved, tile)
            s1[4 * zq + qq] = encode(tile, lse_tile)

    small[5].wait()
    small[6].wait()
    spot = lax.broadcasted_iota(jnp.int32, (32, 128), 1)
    want = lax.broadcasted_iota(jnp.int32, (32, 128), 0) + 32 * (t % 4)
    onehot = jnp.where(spot == want, 1.0, 0.0).astype(BF16)
    rtile = jnp.dot(res_ref[...], onehot, preferred_element_type=F32)
    rsrc[...] = rtile
    rbuf[t] = rtile
    gain32[...] = gain_ref[...].astype(F32).reshape(4, 32, 128)
    zd[3] = s1[z]
    zp[4] = s1[(z + 4) % 16]
    zm[3] = s1[(z + 12) % 16]

    pl.semaphore_wait(barrier, 39)

    def send_z1(src, dst, step, sem):
        pltpu.make_async_remote_copy(
            src_ref=src,
            dst_ref=dst,
            send_sem=send_sems.at[sem],
            recv_sem=recv_sems.at[sem],
            device_id=(y * 16 + (z + step) % 16, t),
            device_id_type=MESH,
        ).start()

    for d in (4, 3, 2, 1):
        send_z1(s1.at[(z + d + 4) % 16], zp.at[d - 1], d, 0)
        if d < 4:
            send_z1(s1.at[(z + 12 - d) % 16], zm.at[d - 1], 16 - d, 6)
    for d in (3, 2, 1):
        send_z1(s1.at[(z + d) % 16], zd.at[3 + d], d, 7)
        send_z1(s1.at[(z + 16 - d) % 16], zd.at[3 - d], 16 - d, 7)

    ow_load.wait()

    def send_w(k):
        py, px, pc = plane_peer(k)
        column = pl.multiple_of(512 * (py * 8 + px * 2 + pc), 512)
        pltpu.make_async_remote_copy(
            src_ref=ow.at[:, pl.ds(column, 512)],
            dst_ref=wbuf.at[slot_ty],
            send_sem=send_sems.at[1],
            recv_sem=recv_sems.at[1],
            device_id=(py * 16 + z, px * 2 + pc),
            device_id_type=MESH,
        ).start()

    loop(W_FIRST, send_w)
    own_column = pl.multiple_of(512 * slot_m, 512)
    own_w = pltpu.make_async_copy(
        ow.at[:, pl.ds(own_column, 512)], wbuf.at[slot_ty], local_sems.at[3]
    )
    own_w.start()

    def send_res(k):
        pltpu.make_async_remote_copy(
            src_ref=rsrc,
            dst_ref=rbuf.at[t],
            send_sem=send_sems.at[2],
            recv_sem=recv_sems.at[2],
            device_id=(j, (t + 1 + k) % 8),
            device_id_type=MESH,
        ).start()

    loop(7, send_res)

    def wait(ref, sem):
        pltpu.make_async_copy(ref, ref, sem).wait()

    wait(zp.at[pl.ds(0, 4)], recv_sems.at[0])
    zrel[0] = encode(*merge(*decode(zp[...])))
    send_z1(zrel.at[0], zfin.at[0], 4, 8)
    wait(zm.at[pl.ds(0, 3)], recv_sems.at[6])
    zrel[1] = encode(*merge(*decode(zm[...])))
    send_z1(zrel.at[1], zfin.at[1], 12, 8)
    loop(W_SECOND, send_w, W_FIRST)
    wait(zd.at[pl.ds(0, 6)], recv_sems.at[7])
    num, top = merge(*decode(zd[...]))
    wait(zfin, recv_sems.at[8])
    nums, tops = decode(zfin[...])
    tile = encode(*merge([num] + nums, [top] + tops))
    psrc[...] = tile
    pbuf[slot_ty] = tile

    def send_p(k):
        py, px, pc = plane_peer(k)
        pltpu.make_async_remote_copy(
            src_ref=psrc,
            dst_ref=pbuf.at[slot_ty],
            send_sem=send_sems.at[3],
            recv_sem=recv_sems.at[3],
            device_id=(py * 16 + z, px * 2 + pc),
            device_id_type=MESH,
        ).start()

    loop(31, send_p)
    loop(31, send_w, W_SECOND)
    wait(pbuf.at[pl.ds(0, 31)], recv_sems.at[3])
    nums, tops = decode(pbuf[...])
    atts = [
        merge(nums[4 * i : 4 * i + 4], tops[4 * i : 4 * i + 4])[0] for i in range(8)
    ]
    att = jnp.concatenate(atts, axis=1).astype(BF16)

    wait(wbuf.at[pl.ds(0, 31)], recv_sems.at[1])
    own_w.wait()
    h_part = jnp.dot(att, wbuf[...].reshape(1024, 512), preferred_element_type=F32)
    wait(rbuf.at[pl.ds(0, 7)], recv_sems.at[2])
    here = z // 2 == t
    r_low = jnp.where(here, rbuf[0] + rbuf[1] + rbuf[2] + rbuf[3], 0.0)
    r_high = jnp.where(here, rbuf[4] + rbuf[5] + rbuf[6] + rbuf[7], 0.0)
    r_both = jnp.concatenate([r_low, r_high], axis=1)
    h_even = h_part[:, 0:256] + jnp.where(z % 2 == 0, r_both, 0.0)
    h_odd = h_part[:, 256:512] + jnp.where(z % 2 == 1, r_both, 0.0)
    h_low = jnp.concatenate([h_even, h_odd], axis=0).astype(BF16)
    z2src[...] = h_low
    z2[z] = h_low

    def send_z2(k):
        kv, tp = z_peer(k)
        pltpu.make_async_remote_copy(
            src_ref=z2src,
            dst_ref=z2.at[z],
            send_sem=send_sems.at[4],
            recv_sem=recv_sems.at[4],
            device_id=(kv, tp),
            device_id_type=MESH,
        ).start()

    loop(15, send_z2)

    lane128 = lax.broadcasted_iota(jnp.int32, (128, 32), 0)
    col32 = lax.broadcasted_iota(jnp.int32, (128, 32), 1)
    mine = jnp.zeros((8, 128), F32)
    for tt in range(8):
        mine = jnp.where(t == tt, atts[tt], mine)
    pick = jnp.where(lane128 == col32 + 32 * y, 1.0, 0.0).astype(BF16)
    att_v[...] = jnp.dot(mine.astype(BF16), pick, preferred_element_type=F32).astype(BF16)

    att_save = pltpu.make_async_copy(att_v, att_out, local_sems.at[11])
    att_save.start()

    wait(z2.at[pl.ds(0, 15)], recv_sems.at[4])
    h_sum = jnp.zeros((16, 256), F32)
    for i in range(16):
        h_sum = h_sum + z2[i].astype(F32)
    h_low = h_sum.astype(BF16)
    hsrc[...] = h_low
    hbuf[slot_m] = h_low

    def send_h(k):
        py, px, pc = plane_peer(k)
        pltpu.make_async_remote_copy(
            src_ref=hsrc,
            dst_ref=hbuf.at[slot_m],
            send_sem=send_sems.at[5],
            recv_sem=h_sems.at[k // 8],
            device_id=(py * 16 + z, px * 2 + pc),
            device_id_type=MESH,
        ).start()

    loop(31, send_h)
    gate_load.wait()
    up_load.wait()
    squares = jnp.zeros((8, 128), F32)
    gate = jnp.zeros((8, 52), F32)
    up = jnp.zeros((8, 52), F32)
    for g, step in enumerate((2, 1, 3, 0)):
        from_y = (y + 4 - step) % 4
        wait(hbuf.at[pl.ds(0, 8 if step else 7)], h_sems.at[g])
        gains = gain32[from_y]
        tiles = []
        for m in range(8):
            full = hbuf[8 * from_y + m].astype(F32)
            for i in range(4):
                r, l = 8 * (i // 2), 128 * (i % 2)
                tile = full[r : r + 8, l : l + 128]
                squares = squares + tile * tile
                tiles.append(tile * gains[4 * m + i : 4 * m + i + 1, :])
        part_h = jnp.concatenate(tiles, axis=1).astype(BF16)
        columns = pl.ds(pl.multiple_of(4096 * from_y, 4096), 4096)
        gate = gate + lax.dot_general(
            part_h, gate_w[:, columns], contract, preferred_element_type=F32
        )
        up = up + lax.dot_general(part_h, up_w[:, columns], contract, preferred_element_type=F32)
    mean = jnp.sum(squares, axis=1, keepdims=True) * (1.0 / 16384)
    inverse = lax.rsqrt(mean + norm_eps)
    gate = gate * inverse
    up = up * inverse
    hid_v[...] = (gate / (1.0 + jnp.exp(-gate)) * up).astype(BF16)
    hid_save = pltpu.make_async_copy(hid_v, hid_out, local_sems.at[12])
    hid_save.start()

    source = hbuf[y * 8 + z // 2].astype(F32)
    half = jnp.where(z % 2 == 0, source[0:8], source[8:16])
    tile = jnp.where(t // 4 == 0, half[:, 0:128], half[:, 128:256])
    pick = jnp.where(lane128 == col32 + 32 * (t % 4), 1.0, 0.0).astype(BF16)
    upd_v[...] = jnp.dot(tile.astype(BF16), pick, preferred_element_type=F32).astype(BF16)
    upd_save = pltpu.make_async_copy(upd_v, upd_out, local_sems.at[13])
    upd_save.start()

    wait(zp.at[pl.ds(0, 4)], send_sems.at[0])
    wait(zm.at[pl.ds(0, 3)], send_sems.at[6])
    wait(zd.at[pl.ds(0, 6)], send_sems.at[7])
    wait(zfin, send_sems.at[8])
    wait(wbuf.at[pl.ds(0, 31)], send_sems.at[1])
    wait(rbuf.at[pl.ds(0, 7)], send_sems.at[2])
    wait(pbuf.at[pl.ds(0, 31)], send_sems.at[3])
    wait(z2.at[pl.ds(0, 15)], send_sems.at[4])
    wait(hbuf.at[pl.ds(0, 31)], send_sems.at[5])
    att_save.wait()
    upd_save.wait()
    hid_save.wait()


def save(a, b, c, a_out, b_out, c_out, sems):
    copies = [
        pltpu.make_async_copy(src, dst, sems.at[i])
        for i, (src, dst) in enumerate(((a, a_out), (b, b_out), (c, c_out)))
    ]
    for copy in copies:
        copy.start()
    for copy in copies:
        copy.wait()


def body(
    queries,
    incoming_keys,
    new_values,
    key_cache,
    value_cache,
    lengths,
    residual,
    norm_gain,
    o_weight,
    gate_weight,
    up_weight,
):
    hbm = pl.BlockSpec(memory_space=pltpu.HBM)
    attended, updated, hidden = pl.pallas_call(
        kernel,
        out_shape=(
            jax.ShapeDtypeStruct((8, 32), BF16),
            jax.ShapeDtypeStruct((8, 32), BF16),
            jax.ShapeDtypeStruct((8, 52), BF16),
        ),
        in_specs=[pl.BlockSpec(memory_space=pltpu.SMEM)] + [hbm] * 10,
        out_specs=(hbm, hbm, hbm),
        scratch_shapes=[
            pltpu.VMEM((8, 2048), BF16),
            pltpu.VMEM((8, 128), BF16),
            pltpu.VMEM((8, 128), BF16),
            pltpu.VMEM((512, 128), BF16),
            pltpu.VMEM((512, 128), BF16),
            pltpu.VMEM((8, 32), BF16),
            pltpu.VMEM((128, 128), BF16),
            pltpu.VMEM((32, 16384), BF16),
            pltpu.VMEM((52, 16384), BF16),
            pltpu.VMEM((52, 16384), BF16),
            pltpu.VMEM((4, 32, 128), F32),
            pltpu.VMEM((16, 16, 128), BF16),
            pltpu.VMEM((7, 16, 128), BF16),
            pltpu.VMEM((5, 16, 128), BF16),
            pltpu.VMEM((4, 16, 128), BF16),
            pltpu.VMEM((2, 16, 128), BF16),
            pltpu.VMEM((2, 16, 128), BF16),
            pltpu.VMEM((8, 128), F32),
            pltpu.VMEM((8, 8, 128), F32),
            pltpu.VMEM((16, 128), BF16),
            pltpu.VMEM((32, 16, 128), BF16),
            pltpu.VMEM((32, 32, 512), BF16),
            pltpu.VMEM((16, 256), BF16),
            pltpu.VMEM((16, 16, 256), BF16),
            pltpu.VMEM((16, 256), BF16),
            pltpu.VMEM((32, 16, 256), BF16),
            pltpu.VMEM((8, 32), BF16),
            pltpu.VMEM((8, 32), BF16),
            pltpu.VMEM((8, 52), BF16),
            pltpu.SemaphoreType.DMA((14,)),
            pltpu.SemaphoreType.DMA((9,)),
            pltpu.SemaphoreType.DMA((9,)),
            pltpu.SemaphoreType.DMA((4,)),
        ],
        compiler_params=pltpu.CompilerParams(
            collective_id=0, has_side_effects=True, vmem_limit_bytes=63 * 1024 * 1024
        ),
        name="decode_layer",
    )(
        lengths,
        queries,
        incoming_keys,
        new_values,
        key_cache.reshape(512, 128),
        value_cache.reshape(512, 128),
        residual,
        norm_gain.reshape(128, 128),
        o_weight.reshape(32, 16384),
        gate_weight,
        up_weight,
    )
    attended, updated, hidden = pl.pallas_call(
        save,
        out_shape=tuple(jax.ShapeDtypeStruct(a.shape, a.dtype) for a in (attended, updated, hidden)),
        in_specs=[hbm] * 3,
        out_specs=(hbm, hbm, hbm),
        scratch_shapes=[pltpu.SemaphoreType.DMA((3,))],
        compiler_params=pltpu.CompilerParams(vmem_limit_bytes=63 * 1024 * 1024),
        name="save_results",
    )(attended, updated, hidden)
    return attended.reshape(8, 1, 32), updated, hidden


def solution(mesh):
    in_specs = (
        P(None, "tp"),
        P(None, "tp"),
        P(None, "tp"),
        P(None, "kvseq", "tp", None),
        P(None, "kvseq", "tp", None),
        P(),
        P(None, ("kvseq", "tp")),
        P(),
        P("tp", "kvseq", None),
        P(("kvseq", "tp"), None),
        P(("kvseq", "tp"), None),
    )
    out_specs = (P(None, "tp", "kvseq"), P(None, ("kvseq", "tp")), P(None, ("kvseq", "tp")))
    return jax.shard_map(body, mesh=mesh, in_specs=in_specs, out_specs=out_specs, check_vma=False)
```

```python
import math

import jax
import jax.numpy as jnp
from jax import lax
from jax.experimental import pallas as pl
from jax.experimental.pallas import tpu as pltpu
from jax.sharding import PartitionSpec as P

norm_eps = 1e-05
MESH = pl.DeviceIdType.MESH
F32, BF16 = jnp.float32, jnp.bfloat16
UNROLL = True
W_FIRST, W_SECOND = 12, 22


def place():
    kv, tp = lax.axis_index("kvseq"), lax.axis_index("tp")
    return kv // 16, kv % 16, tp // 2, tp % 2


def z_peer(k):
    y, z, x, c = place()
    step = jnp.where(k % 2 == 0, 8 + k // 2, 8 - (k + 1) // 2)
    return (y * 16 + (z + step) % 16, x * 2 + c)


def z_near(k):
    y, z, x, c = place()
    step = jnp.where(k % 2 == 0, 4 - k // 2, 12 + k // 2)
    return (y * 16 + (z + step) % 16, x * 2 + c)


def far_first(a):
    return jnp.where(a == 0, 2, jnp.where(a == 1, 1, jnp.where(a == 2, 3, 0)))


def plane_peer(k):
    y, z, x, c = place()
    py = (y + far_first(k // 8)) % 4
    px = (x + far_first((k // 2) % 4)) % 4
    return py, px, (c + 1 - k % 2) % 2


def core_first(k):
    y, z, x, c = place()
    other = k >= 15
    i = jnp.where(other, k - 15, k)
    return (y + far_first(i // 4)) % 4, (x + far_first(i % 4)) % 4, jnp.where(other, 1 - c, c)


def loop(n, body, start=0):
    def step(k, carry):
        body(k)
        return carry

    lax.fori_loop(start, n, step, 0, unroll=UNROLL)


def merge(nums, tops):
    peak = tops[0]
    for top in tops[1:]:
        peak = jnp.maximum(peak, top)
    num, den = 0.0, 0.0
    for part, top in zip(nums, tops):
        w = jnp.exp(top - peak)
        num = num + w * part
        den = den + w
    return num / den, peak + jnp.log(den)


def encode(num, top):
    spot = lax.broadcasted_iota(jnp.int32, (8, 128), 1) % 32
    high = top.astype(BF16).astype(F32)
    middle = (top - high).astype(BF16).astype(F32)
    low = top - high - middle
    terms = jnp.where(spot == 0, high, jnp.where(spot == 1, middle, jnp.where(spot == 2, low, 0.0)))
    return jnp.concatenate([num, terms], axis=0).astype(BF16)


def decode(tiles):
    n = tiles.shape[0]
    a = lax.broadcasted_iota(jnp.int32, (128, 128), 0) // 32
    b = lax.broadcasted_iota(jnp.int32, (128, 128), 1) // 32
    ones = jnp.where(a == b, 1.0, 0.0).astype(BF16)
    sums = jnp.dot(tiles.reshape(16 * n, 128), ones, preferred_element_type=F32)
    values = tiles.astype(F32)
    return [values[i, 0:8] for i in range(n)], [sums[16 * i + 8 : 16 * i + 16] for i in range(n)]


def kernel(
    lengths_ref,
    q_hbm,
    ik_hbm,
    nv_hbm,
    k_hbm,
    v_hbm,
    res_hbm,
    gain_hbm,
    ow_hbm,
    gate_hbm,
    up_hbm,
    att_out,
    upd_out,
    hid_out,
    q_ref,
    ik_ref,
    nv_ref,
    k_ref,
    v_ref,
    res_ref,
    gain_ref,
    ow,
    gate_w,
    up_w,
    gain32,
    s1,
    zd,
    zp,
    zm,
    zrel,
    zfin,
    rsrc,
    rbuf,
    psrc,
    pbuf,
    wbuf,
    z2src,
    z2,
    hsrc,
    hbuf,
    att_v,
    upd_v,
    hid_v,
    local_sems,
    send_sems,
    recv_sems,
    h_sems,
    ready,
):
    y, z, x, c = place()
    t = x * 2 + c
    j = y * 16 + z
    slot_ty = t * 4 + y
    slot_m = y * 8 + t
    barrier = pltpu.get_barrier_semaphore()

    def greet_z(k):
        pl.semaphore_signal(barrier, inc=1, device_id=z_near(k), device_id_type=MESH)

    def greet_plane(k):
        py, px, pc = core_first(k)
        pl.semaphore_signal(
            barrier, inc=1, device_id=(py * 16 + z, px * 2 + pc), device_id_type=MESH
        )

    small = []
    for i, (src, dst) in enumerate(
        (
            (q_hbm, q_ref),
            (k_hbm, k_ref),
            (ik_hbm, ik_ref),
            (v_hbm, v_ref),
            (nv_hbm, nv_ref),
            (res_hbm, res_ref),
            (gain_hbm, gain_ref),
        )
    ):
        small.append(pltpu.make_async_copy(src, dst, local_sems.at[4 + i]))
        if i < 5:
            small[-1].start()
    loop(8, greet_z)
    loop(15, greet_plane)
    partner = (j, x * 2 + 1 - c)
    pl.semaphore_signal(barrier, inc=1, device_id=partner, device_id_type=MESH)
    small[5].start()
    small[6].start()
    ow_load = pltpu.make_async_copy(ow_hbm, ow, local_sems.at[0])
    gate_load = pltpu.make_async_copy(gate_hbm, gate_w, local_sems.at[1])
    up_load = pltpu.make_async_copy(up_hbm, up_w, local_sems.at[2])
    ow_load.start()
    gate_load.start()
    up_load.start()

    for i in range(5):
        small[i].wait()

    scale = 1.0 / math.sqrt(128)
    qs = [q_ref[:, 128 * h : 128 * h + 128].astype(F32) for h in range(16)]
    q_all = jnp.concatenate(qs, axis=0).astype(BF16)
    contract = (((1,), (1,)), ((), ()))
    s_all = lax.dot_general(q_all, k_ref[...], contract, preferred_element_type=F32) * scale
    row = lax.broadcasted_iota(jnp.int32, (8, 512), 0)
    lane = lax.broadcasted_iota(jnp.int32, (8, 512), 1)
    length = jnp.zeros((8, 512), jnp.int32)
    for b in range(8):
        length = jnp.where(row == b, lengths_ref[b], length)
    live = jnp.logical_and(lane // 64 == row, j * 64 + lane % 64 < length)
    ik = ik_ref[...].astype(F32)
    nv = nv_ref[...].astype(F32)
    first = j == 0
    probs, extra, floors, lses = [], [], [], []
    for h in range(16):
        s = s_all[8 * h : 8 * h + 8]
        fresh = jnp.sum(qs[h] * ik, axis=1, keepdims=True) * scale
        fresh = jnp.where(first, fresh, -1e30)
        top = jnp.max(jnp.where(live, s, -10000.0), axis=1, keepdims=True)
        top = jnp.maximum(top, fresh)
        p = jnp.where(live, jnp.exp(s - top), 0.0)
        pnew = jnp.exp(fresh - top)
        floor = jnp.maximum(jnp.sum(p, axis=1, keepdims=True) + pnew, 1.0)
        probs.append(p)
        extra.append(pnew.astype(BF16).astype(F32) * nv)
        floors.append(floor)
        lses.append(top + jnp.log(floor))
    p_all = jnp.concatenate(probs, axis=0).astype(BF16)
    numer = jnp.dot(p_all, v_ref[...], preferred_element_type=F32)
    part = [(numer[8 * h : 8 * h + 8] + extra[h]) / floors[h] for h in range(16)]

    block = lax.broadcasted_iota(jnp.int32, (8, 128), 1) // 32
    for zq in range(4):
        lse_tile = jnp.zeros((8, 128), F32)
        for yy in range(4):
            lse_tile = jnp.where(block == yy, lses[4 * yy + zq], lse_tile)
        for qq in range(4):
            tile = jnp.zeros((8, 128), F32)
            for yy in range(4):
                moved = part[4 * yy + zq]
                shift = (32 * (yy - qq)) % 128
                if shift:
                    moved = pltpu.roll(moved, shift, 1)
                tile = jnp.where(block == yy, moved, tile)
            s1[4 * zq + qq] = encode(tile, lse_tile)

    small[5].wait()
    small[6].wait()
    spot = lax.broadcasted_iota(jnp.int32, (32, 128), 1)
    want = lax.broadcasted_iota(jnp.int32, (32, 128), 0) + 32 * (t % 4)
    onehot = jnp.where(spot == want, 1.0, 0.0).astype(BF16)
    rtile = jnp.dot(res_ref[...], onehot, preferred_element_type=F32)
    rsrc[...] = rtile
    rbuf[t] = rtile
    gain32[...] = gain_ref[...].astype(F32).reshape(4, 32, 128)
    zd[3] = s1[z]
    zp[4] = s1[(z + 4) % 16]
    zm[3] = s1[(z + 12) % 16]

    pl.semaphore_wait(barrier, 24)
    pl.semaphore_signal(ready, inc=1, device_id=partner, device_id_type=MESH)

    def send_z1(src, dst, step, sem):
        pltpu.make_async_remote_copy(
            src_ref=src,
            dst_ref=dst,
            send_sem=send_sems.at[sem],
            recv_sem=recv_sems.at[sem],
            device_id=(y * 16 + (z + step) % 16, t),
            device_id_type=MESH,
        ).start()

    for d in (4, 3, 2, 1):
        send_z1(s1.at[(z + d + 4) % 16], zp.at[d - 1], d, 0)
        if d < 4:
            send_z1(s1.at[(z + 12 - d) % 16], zm.at[d - 1], 16 - d, 6)
    for d in (3, 2, 1):
        send_z1(s1.at[(z + d) % 16], zd.at[3 + d], d, 7)
        send_z1(s1.at[(z + 16 - d) % 16], zd.at[3 - d], 16 - d, 7)

    ow_load.wait()

    def send_w(k):
        py, px, pc = core_first(k)
        column = pl.multiple_of(512 * (py * 8 + px * 2 + pc), 512)
        pltpu.make_async_remote_copy(
            src_ref=ow.at[:, pl.ds(column, 512)],
            dst_ref=wbuf.at[slot_ty],
            send_sem=send_sems.at[1],
            recv_sem=recv_sems.at[1],
            device_id=(py * 16 + z, px * 2 + pc),
            device_id_type=MESH,
        ).start()

    loop(W_FIRST, send_w)
    own_column = pl.multiple_of(512 * slot_m, 512)
    own_w = pltpu.make_async_copy(
        ow.at[:, pl.ds(own_column, 512)], wbuf.at[slot_ty], local_sems.at[3]
    )
    own_w.start()

    def send_res(k):
        pltpu.make_async_remote_copy(
            src_ref=rsrc,
            dst_ref=rbuf.at[t],
            send_sem=send_sems.at[2],
            recv_sem=recv_sems.at[2],
            device_id=(j, (t + 1 + k) % 8),
            device_id_type=MESH,
        ).start()

    pl.semaphore_wait(ready, 1)
    loop(7, send_res)

    def wait(ref, sem):
        pltpu.make_async_copy(ref, ref, sem).wait()

    wait(zp.at[pl.ds(0, 4)], recv_sems.at[0])
    zrel[0] = encode(*merge(*decode(zp[...])))
    send_z1(zrel.at[0], zfin.at[0], 4, 8)
    wait(zm.at[pl.ds(0, 3)], recv_sems.at[6])
    zrel[1] = encode(*merge(*decode(zm[...])))
    send_z1(zrel.at[1], zfin.at[1], 12, 8)
    loop(W_SECOND, send_w, W_FIRST)
    wait(zd.at[pl.ds(0, 6)], recv_sems.at[7])
    num, top = merge(*decode(zd[...]))
    wait(zfin, recv_sems.at[8])
    nums, tops = decode(zfin[...])
    tile = encode(*merge([num] + nums, [top] + tops))
    psrc[...] = tile
    pbuf[slot_ty] = tile

    def send_p(k):
        py, px, pc = plane_peer(k)
        pltpu.make_async_remote_copy(
            src_ref=psrc,
            dst_ref=pbuf.at[slot_ty],
            send_sem=send_sems.at[3],
            recv_sem=recv_sems.at[3],
            device_id=(py * 16 + z, px * 2 + pc),
            device_id_type=MESH,
        ).start()

    loop(31, send_p)
    loop(31, send_w, W_SECOND)
    wait(pbuf.at[pl.ds(0, 31)], recv_sems.at[3])
    nums, tops = decode(pbuf[...])
    atts = [
        merge(nums[4 * i : 4 * i + 4], tops[4 * i : 4 * i + 4])[0] for i in range(8)
    ]
    att = jnp.concatenate(atts, axis=1).astype(BF16)

    wait(wbuf.at[pl.ds(0, 31)], recv_sems.at[1])
    own_w.wait()
    h_part = jnp.dot(att, wbuf[...].reshape(1024, 512), preferred_element_type=F32)
    wait(rbuf.at[pl.ds(0, 7)], recv_sems.at[2])
    here = z // 2 == t
    r_low = jnp.where(here, rbuf[0] + rbuf[1] + rbuf[2] + rbuf[3], 0.0)
    r_high = jnp.where(here, rbuf[4] + rbuf[5] + rbuf[6] + rbuf[7], 0.0)
    r_both = jnp.concatenate([r_low, r_high], axis=1)
    h_even = h_part[:, 0:256] + jnp.where(z % 2 == 0, r_both, 0.0)
    h_odd = h_part[:, 256:512] + jnp.where(z % 2 == 1, r_both, 0.0)
    h_low = jnp.concatenate([h_even, h_odd], axis=0).astype(BF16)
    z2src[...] = h_low
    z2[z] = h_low

    def send_z2(k):
        kv, tp = z_peer(k)
        pltpu.make_async_remote_copy(
            src_ref=z2src,
            dst_ref=z2.at[z],
            send_sem=send_sems.at[4],
            recv_sem=recv_sems.at[4],
            device_id=(kv, tp),
            device_id_type=MESH,
        ).start()

    loop(15, send_z2)

    lane128 = lax.broadcasted_iota(jnp.int32, (128, 32), 0)
    col32 = lax.broadcasted_iota(jnp.int32, (128, 32), 1)
    mine = jnp.zeros((8, 128), F32)
    for tt in range(8):
        mine = jnp.where(t == tt, atts[tt], mine)
    pick = jnp.where(lane128 == col32 + 32 * y, 1.0, 0.0).astype(BF16)
    att_v[...] = jnp.dot(mine.astype(BF16), pick, preferred_element_type=F32).astype(BF16)

    att_save = pltpu.make_async_copy(att_v, att_out, local_sems.at[11])
    att_save.start()

    wait(z2.at[pl.ds(0, 15)], recv_sems.at[4])
    h_sum = jnp.zeros((16, 256), F32)
    for i in range(16):
        h_sum = h_sum + z2[i].astype(F32)
    h_low = h_sum.astype(BF16)
    hsrc[...] = h_low
    hbuf[slot_m] = h_low

    def send_h(k):
        py, px, pc = plane_peer(k)
        pltpu.make_async_remote_copy(
            src_ref=hsrc,
            dst_ref=hbuf.at[slot_m],
            send_sem=send_sems.at[5],
            recv_sem=h_sems.at[k // 8],
            device_id=(py * 16 + z, px * 2 + pc),
            device_id_type=MESH,
        ).start()

    loop(31, send_h)
    gate_load.wait()
    up_load.wait()
    squares = jnp.zeros((8, 128), F32)
    gate = jnp.zeros((8, 52), F32)
    up = jnp.zeros((8, 52), F32)
    for g, step in enumerate((2, 1, 3, 0)):
        from_y = (y + 4 - step) % 4
        wait(hbuf.at[pl.ds(0, 8 if step else 7)], h_sems.at[g])
        gains = gain32[from_y]
        tiles = []
        for m in range(8):
            full = hbuf[8 * from_y + m].astype(F32)
            for i in range(4):
                r, l = 8 * (i // 2), 128 * (i % 2)
                tile = full[r : r + 8, l : l + 128]
                squares = squares + tile * tile
                tiles.append(tile * gains[4 * m + i : 4 * m + i + 1, :])
        part_h = jnp.concatenate(tiles, axis=1).astype(BF16)
        columns = pl.ds(pl.multiple_of(4096 * from_y, 4096), 4096)
        gate = gate + lax.dot_general(
            part_h, gate_w[:, columns], contract, preferred_element_type=F32
        )
        up = up + lax.dot_general(part_h, up_w[:, columns], contract, preferred_element_type=F32)
    source = hbuf[y * 8 + z // 2].astype(F32)
    half = jnp.where(z % 2 == 0, source[0:8], source[8:16])
    tile = jnp.where(t // 4 == 0, half[:, 0:128], half[:, 128:256])
    pick = jnp.where(lane128 == col32 + 32 * (t % 4), 1.0, 0.0).astype(BF16)
    upd_v[...] = jnp.dot(tile.astype(BF16), pick, preferred_element_type=F32).astype(BF16)
    upd_save = pltpu.make_async_copy(upd_v, upd_out, local_sems.at[13])
    upd_save.start()

    mean = jnp.sum(squares, axis=1, keepdims=True) * (1.0 / 16384)
    inverse = lax.rsqrt(mean + norm_eps)
    gate = gate * inverse
    up = up * inverse
    hid_v[...] = (gate / (1.0 + jnp.exp(-gate)) * up).astype(BF16)
    hid_save = pltpu.make_async_copy(hid_v, hid_out, local_sems.at[12])
    hid_save.start()

    wait(zp.at[pl.ds(0, 4)], send_sems.at[0])
    wait(zm.at[pl.ds(0, 3)], send_sems.at[6])
    wait(zd.at[pl.ds(0, 6)], send_sems.at[7])
    wait(zfin, send_sems.at[8])
    wait(wbuf.at[pl.ds(0, 31)], send_sems.at[1])
    wait(rbuf.at[pl.ds(0, 7)], send_sems.at[2])
    wait(pbuf.at[pl.ds(0, 31)], send_sems.at[3])
    wait(z2.at[pl.ds(0, 15)], send_sems.at[4])
    wait(hbuf.at[pl.ds(0, 31)], send_sems.at[5])
    att_save.wait()
    upd_save.wait()
    hid_save.wait()


def save(a, b, c, a_out, b_out, c_out, sems):
    copies = [
        pltpu.make_async_copy(src, dst, sems.at[i])
        for i, (src, dst) in enumerate(((a, a_out), (b, b_out), (c, c_out)))
    ]
    for copy in copies:
        copy.start()
    for copy in copies:
        copy.wait()


def body(
    queries,
    incoming_keys,
    new_values,
    key_cache,
    value_cache,
    lengths,
    residual,
    norm_gain,
    o_weight,
    gate_weight,
    up_weight,
):
    hbm = pl.BlockSpec(memory_space=pltpu.HBM)
    attended, updated, hidden = pl.pallas_call(
        kernel,
        out_shape=(
            jax.ShapeDtypeStruct((8, 32), BF16),
            jax.ShapeDtypeStruct((8, 32), BF16),
            jax.ShapeDtypeStruct((8, 52), BF16),
        ),
        in_specs=[pl.BlockSpec(memory_space=pltpu.SMEM)] + [hbm] * 10,
        out_specs=(hbm, hbm, hbm),
        scratch_shapes=[
            pltpu.VMEM((8, 2048), BF16),
            pltpu.VMEM((8, 128), BF16),
            pltpu.VMEM((8, 128), BF16),
            pltpu.VMEM((512, 128), BF16),
            pltpu.VMEM((512, 128), BF16),
            pltpu.VMEM((8, 32), BF16),
            pltpu.VMEM((128, 128), BF16),
            pltpu.VMEM((32, 16384), BF16),
            pltpu.VMEM((52, 16384), BF16),
            pltpu.VMEM((52, 16384), BF16),
            pltpu.VMEM((4, 32, 128), F32),
            pltpu.VMEM((16, 16, 128), BF16),
            pltpu.VMEM((7, 16, 128), BF16),
            pltpu.VMEM((5, 16, 128), BF16),
            pltpu.VMEM((4, 16, 128), BF16),
            pltpu.VMEM((2, 16, 128), BF16),
            pltpu.VMEM((2, 16, 128), BF16),
            pltpu.VMEM((8, 128), F32),
            pltpu.VMEM((8, 8, 128), F32),
            pltpu.VMEM((16, 128), BF16),
            pltpu.VMEM((32, 16, 128), BF16),
            pltpu.VMEM((32, 32, 512), BF16),
            pltpu.VMEM((16, 256), BF16),
            pltpu.VMEM((16, 16, 256), BF16),
            pltpu.VMEM((16, 256), BF16),
            pltpu.VMEM((32, 16, 256), BF16),
            pltpu.VMEM((8, 32), BF16),
            pltpu.VMEM((8, 32), BF16),
            pltpu.VMEM((8, 52), BF16),
            pltpu.SemaphoreType.DMA((14,)),
            pltpu.SemaphoreType.DMA((9,)),
            pltpu.SemaphoreType.DMA((9,)),
            pltpu.SemaphoreType.DMA((4,)),
            pltpu.SemaphoreType.REGULAR,
        ],
        compiler_params=pltpu.CompilerParams(
            collective_id=0, has_side_effects=True, vmem_limit_bytes=63 * 1024 * 1024
        ),
        name="decode_layer",
    )(
        lengths,
        queries,
        incoming_keys,
        new_values,
        key_cache.reshape(512, 128),
        value_cache.reshape(512, 128),
        residual,
        norm_gain.reshape(128, 128),
        o_weight.reshape(32, 16384),
        gate_weight,
        up_weight,
    )
    attended, updated, hidden = pl.pallas_call(
        save,
        out_shape=tuple(jax.ShapeDtypeStruct(a.shape, a.dtype) for a in (attended, updated, hidden)),
        in_specs=[hbm] * 3,
        out_specs=(hbm, hbm, hbm),
        scratch_shapes=[pltpu.SemaphoreType.DMA((3,))],
        compiler_params=pltpu.CompilerParams(vmem_limit_bytes=63 * 1024 * 1024),
        name="save_results",
    )(attended, updated, hidden)
    return attended.reshape(8, 1, 32), updated, hidden


def solution(mesh):
    in_specs = (
        P(None, "tp"),
        P(None, "tp"),
        P(None, "tp"),
        P(None, "kvseq", "tp", None),
        P(None, "kvseq", "tp", None),
        P(),
        P(None, ("kvseq", "tp")),
        P(),
        P("tp", "kvseq", None),
        P(("kvseq", "tp"), None),
        P(("kvseq", "tp"), None),
    )
    out_specs = (P(None, "tp", "kvseq"), P(None, ("kvseq", "tp")), P(None, ("kvseq", "tp")))
    return jax.shard_map(body, mesh=mesh, in_specs=in_specs, out_specs=out_specs, check_vma=False)
```

```python
import math

import jax
import jax.numpy as jnp
from jax import lax
from jax.experimental import pallas as pl
from jax.experimental.pallas import tpu as pltpu
from jax.sharding import PartitionSpec as P

norm_eps = 1e-05
MESH = pl.DeviceIdType.MESH
F32, BF16 = jnp.float32, jnp.bfloat16
UNROLL = True
W_FIRST, W_SECOND = 12, 22


def place():
    kv, tp = lax.axis_index("kvseq"), lax.axis_index("tp")
    return kv // 16, kv % 16, tp // 2, tp % 2


def z_peer(k):
    y, z, x, c = place()
    step = jnp.where(k % 2 == 0, 8 + k // 2, 8 - (k + 1) // 2)
    return (y * 16 + (z + step) % 16, x * 2 + c)


def z_near(k):
    y, z, x, c = place()
    step = jnp.where(k % 2 == 0, 4 - k // 2, 12 + k // 2)
    return (y * 16 + (z + step) % 16, x * 2 + c)


def far_first(a):
    return jnp.where(a == 0, 2, jnp.where(a == 1, 1, jnp.where(a == 2, 3, 0)))


def plane_peer(k):
    y, z, x, c = place()
    py = (y + far_first(k // 8)) % 4
    px = (x + far_first((k // 2) % 4)) % 4
    return py, px, (c + 1 - k % 2) % 2


def core_first(k):
    y, z, x, c = place()
    other = k >= 15
    i = jnp.where(other, k - 15, k)
    return (y + far_first(i // 4)) % 4, (x + far_first(i % 4)) % 4, jnp.where(other, 1 - c, c)


def loop(n, body, start=0):
    def step(k, carry):
        body(k)
        return carry

    lax.fori_loop(start, n, step, 0, unroll=UNROLL)


def merge(nums, tops):
    peak = tops[0]
    for top in tops[1:]:
        peak = jnp.maximum(peak, top)
    num, den = 0.0, 0.0
    for part, top in zip(nums, tops):
        w = jnp.exp(top - peak)
        num = num + w * part
        den = den + w
    return num / den, peak + jnp.log(den)


def encode(num, top):
    spot = lax.broadcasted_iota(jnp.int32, (8, 128), 1) % 32
    high = top.astype(BF16).astype(F32)
    middle = (top - high).astype(BF16).astype(F32)
    low = top - high - middle
    terms = jnp.where(spot == 0, high, jnp.where(spot == 1, middle, jnp.where(spot == 2, low, 0.0)))
    return jnp.concatenate([num, terms], axis=0).astype(BF16)


def decode(tiles):
    n = tiles.shape[0]
    a = lax.broadcasted_iota(jnp.int32, (128, 128), 0) // 32
    b = lax.broadcasted_iota(jnp.int32, (128, 128), 1) // 32
    ones = jnp.where(a == b, 1.0, 0.0).astype(BF16)
    sums = jnp.dot(tiles.reshape(16 * n, 128), ones, preferred_element_type=F32)
    values = tiles.astype(F32)
    return [values[i, 0:8] for i in range(n)], [sums[16 * i + 8 : 16 * i + 16] for i in range(n)]


def kernel(
    lengths_ref,
    q_hbm,
    ik_hbm,
    nv_hbm,
    k_hbm,
    v_hbm,
    res_hbm,
    gain_hbm,
    ow_hbm,
    gate_hbm,
    up_hbm,
    att_out,
    upd_out,
    hid_out,
    q_ref,
    ik_ref,
    nv_ref,
    k_ref,
    v_ref,
    res_ref,
    gain_ref,
    ow,
    gate_w,
    up_w,
    gain32,
    s1,
    zd,
    zp,
    zm,
    zrel,
    zfin,
    rsrc,
    rbuf,
    psrc,
    pbuf,
    wbuf,
    z2src,
    z2,
    hsrc,
    hbuf,
    att_v,
    upd_v,
    hid_v,
    local_sems,
    send_sems,
    recv_sems,
    h_sems,
    ready,
):
    y, z, x, c = place()
    t = x * 2 + c
    j = y * 16 + z
    slot_ty = t * 4 + y
    slot_m = y * 8 + t
    barrier = pltpu.get_barrier_semaphore()

    def greet_z(k):
        pl.semaphore_signal(barrier, inc=1, device_id=z_near(k), device_id_type=MESH)

    def greet_plane(k):
        py, px, pc = core_first(k)
        pl.semaphore_signal(
            barrier, inc=1, device_id=(py * 16 + z, px * 2 + pc), device_id_type=MESH
        )

    small = []
    for i, (src, dst) in enumerate(
        (
            (q_hbm, q_ref),
            (k_hbm, k_ref),
            (ik_hbm, ik_ref),
            (v_hbm, v_ref),
            (nv_hbm, nv_ref),
            (res_hbm, res_ref),
            (gain_hbm, gain_ref),
        )
    ):
        small.append(pltpu.make_async_copy(src, dst, local_sems.at[4 + i]))
        if i < 5:
            small[-1].start()
    loop(8, greet_z)
    loop(15, greet_plane)
    partner = (j, x * 2 + 1 - c)
    pl.semaphore_signal(barrier, inc=1, device_id=partner, device_id_type=MESH)
    small[5].start()
    small[6].start()
    ow_load = pltpu.make_async_copy(ow_hbm, ow, local_sems.at[0])
    gate_load = pltpu.make_async_copy(gate_hbm, gate_w, local_sems.at[1])
    up_load = pltpu.make_async_copy(up_hbm, up_w, local_sems.at[2])
    ow_load.start()
    gate_load.start()
    up_load.start()

    for i in range(5):
        small[i].wait()

    scale = 1.0 / math.sqrt(128)
    qs = [q_ref[:, 128 * h : 128 * h + 128].astype(F32) for h in range(16)]
    q_all = jnp.concatenate(qs, axis=0).astype(BF16)
    contract = (((1,), (1,)), ((), ()))
    s_all = lax.dot_general(q_all, k_ref[...], contract, preferred_element_type=F32) * scale
    row = lax.broadcasted_iota(jnp.int32, (8, 512), 0)
    lane = lax.broadcasted_iota(jnp.int32, (8, 512), 1)
    length = jnp.zeros((8, 512), jnp.int32)
    for b in range(8):
        length = jnp.where(row == b, lengths_ref[b], length)
    live = jnp.logical_and(lane // 64 == row, j * 64 + lane % 64 < length)
    ik = ik_ref[...].astype(F32)
    nv = nv_ref[...].astype(F32)
    first = j == 0
    probs, extra, floors, lses = [], [], [], []
    for h in range(16):
        s = s_all[8 * h : 8 * h + 8]
        fresh = jnp.sum(qs[h] * ik, axis=1, keepdims=True) * scale
        fresh = jnp.where(first, fresh, -1e30)
        top = jnp.max(jnp.where(live, s, -10000.0), axis=1, keepdims=True)
        top = jnp.maximum(top, fresh)
        p = jnp.where(live, jnp.exp(s - top), 0.0)
        pnew = jnp.exp(fresh - top)
        floor = jnp.maximum(jnp.sum(p, axis=1, keepdims=True) + pnew, 1.0)
        probs.append(p)
        extra.append(pnew.astype(BF16).astype(F32) * nv)
        floors.append(floor)
        lses.append(top + jnp.log(floor))
    p_all = jnp.concatenate(probs, axis=0).astype(BF16)
    numer = jnp.dot(p_all, v_ref[...], preferred_element_type=F32)
    part = [(numer[8 * h : 8 * h + 8] + extra[h]) / floors[h] for h in range(16)]

    block = lax.broadcasted_iota(jnp.int32, (8, 128), 1) // 32
    for zq in range(4):
        lse_tile = jnp.zeros((8, 128), F32)
        for yy in range(4):
            lse_tile = jnp.where(block == yy, lses[4 * yy + zq], lse_tile)
        for qq in range(4):
            tile = jnp.zeros((8, 128), F32)
            for yy in range(4):
                moved = part[4 * yy + zq]
                shift = (32 * (yy - qq)) % 128
                if shift:
                    moved = pltpu.roll(moved, shift, 1)
                tile = jnp.where(block == yy, moved, tile)
            s1[4 * zq + qq] = encode(tile, lse_tile)

    small[5].wait()
    small[6].wait()
    spot = lax.broadcasted_iota(jnp.int32, (32, 128), 1)
    want = lax.broadcasted_iota(jnp.int32, (32, 128), 0) + 32 * (t % 4)
    onehot = jnp.where(spot == want, 1.0, 0.0).astype(BF16)
    rtile = jnp.dot(res_ref[...], onehot, preferred_element_type=F32)
    rsrc[...] = rtile
    rbuf[t] = rtile
    gain32[...] = gain_ref[...].astype(F32).reshape(4, 32, 128)
    zd[3] = s1[z]
    zp[4] = s1[(z + 4) % 16]
    zm[3] = s1[(z + 12) % 16]

    pl.semaphore_wait(barrier, 24)
    pl.semaphore_signal(ready, inc=1, device_id=partner, device_id_type=MESH)

    def send_z1(src, dst, step, sem):
        pltpu.make_async_remote_copy(
            src_ref=src,
            dst_ref=dst,
            send_sem=send_sems.at[sem],
            recv_sem=recv_sems.at[sem],
            device_id=(y * 16 + (z + step) % 16, t),
            device_id_type=MESH,
        ).start()

    for d in (4, 3, 2, 1):
        send_z1(s1.at[(z + d + 4) % 16], zp.at[d - 1], d, 0)
        if d < 4:
            send_z1(s1.at[(z + 12 - d) % 16], zm.at[d - 1], 16 - d, 6)
    for d in (3, 2, 1):
        send_z1(s1.at[(z + d) % 16], zd.at[3 + d], d, 7)
        send_z1(s1.at[(z + 16 - d) % 16], zd.at[3 - d], 16 - d, 7)

    ow_load.wait()

    def send_w(k):
        py, px, pc = core_first(k)
        column = pl.multiple_of(512 * (py * 8 + px * 2 + pc), 512)
        pltpu.make_async_remote_copy(
            src_ref=ow.at[:, pl.ds(column, 512)],
            dst_ref=wbuf.at[slot_ty],
            send_sem=send_sems.at[1],
            recv_sem=recv_sems.at[1],
            device_id=(py * 16 + z, px * 2 + pc),
            device_id_type=MESH,
        ).start()

    loop(W_FIRST, send_w)
    own_column = pl.multiple_of(512 * slot_m, 512)
    own_w = pltpu.make_async_copy(
        ow.at[:, pl.ds(own_column, 512)], wbuf.at[slot_ty], local_sems.at[3]
    )
    own_w.start()

    def send_res(k):
        pltpu.make_async_remote_copy(
            src_ref=rsrc,
            dst_ref=rbuf.at[t],
            send_sem=send_sems.at[2],
            recv_sem=recv_sems.at[2],
            device_id=(j, (t + 1 + k) % 8),
            device_id_type=MESH,
        ).start()

    pl.semaphore_wait(ready, 1)
    loop(7, send_res)

    def wait(ref, sem):
        pltpu.make_async_copy(ref, ref, sem).wait()

    wait(zp.at[pl.ds(0, 4)], recv_sems.at[0])
    zrel[0] = encode(*merge(*decode(zp[...])))
    send_z1(zrel.at[0], zfin.at[0], 4, 8)
    wait(zm.at[pl.ds(0, 3)], recv_sems.at[6])
    zrel[1] = encode(*merge(*decode(zm[...])))
    send_z1(zrel.at[1], zfin.at[1], 12, 8)
    loop(W_SECOND, send_w, W_FIRST)
    wait(zd.at[pl.ds(0, 6)], recv_sems.at[7])
    num, top = merge(*decode(zd[...]))
    wait(zfin, recv_sems.at[8])
    nums, tops = decode(zfin[...])
    tile = encode(*merge([num] + nums, [top] + tops))
    psrc[...] = tile
    pbuf[slot_ty] = tile

    def send_p(k):
        py, px, pc = plane_peer(k)
        pltpu.make_async_remote_copy(
            src_ref=psrc,
            dst_ref=pbuf.at[slot_ty],
            send_sem=send_sems.at[3],
            recv_sem=recv_sems.at[3],
            device_id=(py * 16 + z, px * 2 + pc),
            device_id_type=MESH,
        ).start()

    loop(31, send_p)
    loop(31, send_w, W_SECOND)
    wait(pbuf.at[pl.ds(0, 31)], recv_sems.at[3])
    nums, tops = decode(pbuf[...])
    atts = [
        merge(nums[4 * i : 4 * i + 4], tops[4 * i : 4 * i + 4])[0] for i in range(8)
    ]
    att = jnp.concatenate(atts, axis=1).astype(BF16)

    wait(wbuf.at[pl.ds(0, 31)], recv_sems.at[1])
    own_w.wait()
    h_part = jnp.dot(att, wbuf[...].reshape(1024, 512), preferred_element_type=F32)
    wait(rbuf.at[pl.ds(0, 7)], recv_sems.at[2])
    here = z // 2 == t
    r_low = jnp.where(here, rbuf[0] + rbuf[1] + rbuf[2] + rbuf[3], 0.0)
    r_high = jnp.where(here, rbuf[4] + rbuf[5] + rbuf[6] + rbuf[7], 0.0)
    r_both = jnp.concatenate([r_low, r_high], axis=1)
    h_even = h_part[:, 0:256] + jnp.where(z % 2 == 0, r_both, 0.0)
    h_odd = h_part[:, 256:512] + jnp.where(z % 2 == 1, r_both, 0.0)
    h_low = jnp.concatenate([h_even, h_odd], axis=0).astype(BF16)
    z2src[...] = h_low
    z2[z] = h_low

    def send_z2(k):
        kv, tp = z_peer(k)
        pltpu.make_async_remote_copy(
            src_ref=z2src,
            dst_ref=z2.at[z],
            send_sem=send_sems.at[4],
            recv_sem=recv_sems.at[4],
            device_id=(kv, tp),
            device_id_type=MESH,
        ).start()

    loop(15, send_z2)

    lane128 = lax.broadcasted_iota(jnp.int32, (128, 32), 0)
    col32 = lax.broadcasted_iota(jnp.int32, (128, 32), 1)
    mine = jnp.zeros((8, 128), F32)
    for tt in range(8):
        mine = jnp.where(t == tt, atts[tt], mine)
    pick = jnp.where(lane128 == col32 + 32 * y, 1.0, 0.0).astype(BF16)
    att_v[...] = jnp.dot(mine.astype(BF16), pick, preferred_element_type=F32).astype(BF16)

    att_save = pltpu.make_async_copy(att_v, att_out, local_sems.at[11])
    att_save.start()

    wait(z2.at[pl.ds(0, 15)], recv_sems.at[4])
    h_sum = jnp.zeros((16, 256), F32)
    for i in range(16):
        h_sum = h_sum + z2[i].astype(F32)
    h_low = h_sum.astype(BF16)
    hsrc[...] = h_low
    hbuf[slot_m] = h_low

    def send_h(k):
        py, px, pc = plane_peer(k)
        pltpu.make_async_remote_copy(
            src_ref=hsrc,
            dst_ref=hbuf.at[slot_m],
            send_sem=send_sems.at[5],
            recv_sem=h_sems.at[k // 8],
            device_id=(py * 16 + z, px * 2 + pc),
            device_id_type=MESH,
        ).start()

    loop(31, send_h)
    gate_load.wait()
    up_load.wait()
    squares = jnp.zeros((8, 128), F32)
    gate = jnp.zeros((8, 52), F32)
    up = jnp.zeros((8, 52), F32)
    for g, step in ((3, 0), (2, 3), (1, 1), (0, 2)):
        from_y = (y + 4 - step) % 4
        wait(hbuf.at[pl.ds(0, 8 if step else 7)], h_sems.at[g])
        gains = gain32[from_y]
        tiles = []
        for m in range(8):
            full = hbuf[8 * from_y + m].astype(F32)
            for i in range(4):
                r, l = 8 * (i // 2), 128 * (i % 2)
                tile = full[r : r + 8, l : l + 128]
                squares = squares + tile * tile
                tiles.append(tile * gains[4 * m + i : 4 * m + i + 1, :])
        part_h = jnp.concatenate(tiles, axis=1).astype(BF16)
        columns = pl.ds(pl.multiple_of(4096 * from_y, 4096), 4096)
        gate = gate + lax.dot_general(
            part_h, gate_w[:, columns], contract, preferred_element_type=F32
        )
        up = up + lax.dot_general(part_h, up_w[:, columns], contract, preferred_element_type=F32)
    source = hbuf[y * 8 + z // 2].astype(F32)
    half = jnp.where(z % 2 == 0, source[0:8], source[8:16])
    tile = jnp.where(t // 4 == 0, half[:, 0:128], half[:, 128:256])
    pick = jnp.where(lane128 == col32 + 32 * (t % 4), 1.0, 0.0).astype(BF16)
    upd_v[...] = jnp.dot(tile.astype(BF16), pick, preferred_element_type=F32).astype(BF16)
    upd_save = pltpu.make_async_copy(upd_v, upd_out, local_sems.at[13])
    upd_save.start()

    mean = jnp.sum(squares, axis=1, keepdims=True) * (1.0 / 16384)
    inverse = lax.rsqrt(mean + norm_eps)
    gate = gate * inverse
    up = up * inverse
    hid_v[...] = (gate / (1.0 + jnp.exp(-gate)) * up).astype(BF16)
    hid_save = pltpu.make_async_copy(hid_v, hid_out, local_sems.at[12])
    hid_save.start()

    wait(zp.at[pl.ds(0, 4)], send_sems.at[0])
    wait(zm.at[pl.ds(0, 3)], send_sems.at[6])
    wait(zd.at[pl.ds(0, 6)], send_sems.at[7])
    wait(zfin, send_sems.at[8])
    wait(wbuf.at[pl.ds(0, 31)], send_sems.at[1])
    wait(rbuf.at[pl.ds(0, 7)], send_sems.at[2])
    wait(pbuf.at[pl.ds(0, 31)], send_sems.at[3])
    wait(z2.at[pl.ds(0, 15)], send_sems.at[4])
    wait(hbuf.at[pl.ds(0, 31)], send_sems.at[5])
    att_save.wait()
    upd_save.wait()
    hid_save.wait()


def save(a, b, c, a_out, b_out, c_out, sems):
    copies = [
        pltpu.make_async_copy(src, dst, sems.at[i])
        for i, (src, dst) in enumerate(((a, a_out), (b, b_out), (c, c_out)))
    ]
    for copy in copies:
        copy.start()
    for copy in copies:
        copy.wait()


def body(
    queries,
    incoming_keys,
    new_values,
    key_cache,
    value_cache,
    lengths,
    residual,
    norm_gain,
    o_weight,
    gate_weight,
    up_weight,
):
    hbm = pl.BlockSpec(memory_space=pltpu.HBM)
    attended, updated, hidden = pl.pallas_call(
        kernel,
        out_shape=(
            jax.ShapeDtypeStruct((8, 32), BF16),
            jax.ShapeDtypeStruct((8, 32), BF16),
            jax.ShapeDtypeStruct((8, 52), BF16),
        ),
        in_specs=[pl.BlockSpec(memory_space=pltpu.SMEM)] + [hbm] * 10,
        out_specs=(hbm, hbm, hbm),
        scratch_shapes=[
            pltpu.VMEM((8, 2048), BF16),
            pltpu.VMEM((8, 128), BF16),
            pltpu.VMEM((8, 128), BF16),
            pltpu.VMEM((512, 128), BF16),
            pltpu.VMEM((512, 128), BF16),
            pltpu.VMEM((8, 32), BF16),
            pltpu.VMEM((128, 128), BF16),
            pltpu.VMEM((32, 16384), BF16),
            pltpu.VMEM((52, 16384), BF16),
            pltpu.VMEM((52, 16384), BF16),
            pltpu.VMEM((4, 32, 128), F32),
            pltpu.VMEM((16, 16, 128), BF16),
            pltpu.VMEM((7, 16, 128), BF16),
            pltpu.VMEM((5, 16, 128), BF16),
            pltpu.VMEM((4, 16, 128), BF16),
            pltpu.VMEM((2, 16, 128), BF16),
            pltpu.VMEM((2, 16, 128), BF16),
            pltpu.VMEM((8, 128), F32),
            pltpu.VMEM((8, 8, 128), F32),
            pltpu.VMEM((16, 128), BF16),
            pltpu.VMEM((32, 16, 128), BF16),
            pltpu.VMEM((32, 32, 512), BF16),
            pltpu.VMEM((16, 256), BF16),
            pltpu.VMEM((16, 16, 256), BF16),
            pltpu.VMEM((16, 256), BF16),
            pltpu.VMEM((32, 16, 256), BF16),
            pltpu.VMEM((8, 32), BF16),
            pltpu.VMEM((8, 32), BF16),
            pltpu.VMEM((8, 52), BF16),
            pltpu.SemaphoreType.DMA((14,)),
            pltpu.SemaphoreType.DMA((9,)),
            pltpu.SemaphoreType.DMA((9,)),
            pltpu.SemaphoreType.DMA((4,)),
            pltpu.SemaphoreType.REGULAR,
        ],
        compiler_params=pltpu.CompilerParams(
            collective_id=0, has_side_effects=True, vmem_limit_bytes=63 * 1024 * 1024
        ),
        name="decode_layer",
    )(
        lengths,
        queries,
        incoming_keys,
        new_values,
        key_cache.reshape(512, 128),
        value_cache.reshape(512, 128),
        residual,
        norm_gain.reshape(128, 128),
        o_weight.reshape(32, 16384),
        gate_weight,
        up_weight,
    )
    attended, updated, hidden = pl.pallas_call(
        save,
        out_shape=tuple(jax.ShapeDtypeStruct(a.shape, a.dtype) for a in (attended, updated, hidden)),
        in_specs=[hbm] * 3,
        out_specs=(hbm, hbm, hbm),
        scratch_shapes=[pltpu.SemaphoreType.DMA((3,))],
        compiler_params=pltpu.CompilerParams(vmem_limit_bytes=63 * 1024 * 1024),
        name="save_results",
    )(attended, updated, hidden)
    return attended.reshape(8, 1, 32), updated, hidden


def solution(mesh):
    in_specs = (
        P(None, "tp"),
        P(None, "tp"),
        P(None, "tp"),
        P(None, "kvseq", "tp", None),
        P(None, "kvseq", "tp", None),
        P(),
        P(None, ("kvseq", "tp")),
        P(),
        P("tp", "kvseq", None),
        P(("kvseq", "tp"), None),
        P(("kvseq", "tp"), None),
    )
    out_specs = (P(None, "tp", "kvseq"), P(None, ("kvseq", "tp")), P(None, ("kvseq", "tp")))
    return jax.shard_map(body, mesh=mesh, in_specs=in_specs, out_specs=out_specs, check_vma=False)
```

```python
import math

import jax
import jax.numpy as jnp
from jax import lax
from jax.experimental import pallas as pl
from jax.experimental.pallas import tpu as pltpu
from jax.sharding import PartitionSpec as P

norm_eps = 1e-05
MESH = pl.DeviceIdType.MESH
F32, BF16 = jnp.float32, jnp.bfloat16
UNROLL = True
W_FIRST, W_SECOND = 12, 22


def place():
    kv, tp = lax.axis_index("kvseq"), lax.axis_index("tp")
    return kv // 16, kv % 16, tp // 2, tp % 2


def z_peer(k):
    y, z, x, c = place()
    step = jnp.where(k % 2 == 0, 8 + k // 2, 8 - (k + 1) // 2)
    return (y * 16 + (z + step) % 16, x * 2 + c)


def z_near(k):
    y, z, x, c = place()
    step = jnp.where(k % 2 == 0, 4 - k // 2, 12 + k // 2)
    return (y * 16 + (z + step) % 16, x * 2 + c)


def far_first(a):
    return jnp.where(a == 0, 2, jnp.where(a == 1, 1, jnp.where(a == 2, 3, 0)))


def plane_peer(k):
    y, z, x, c = place()
    py = (y + far_first(k // 8)) % 4
    px = (x + far_first((k // 2) % 4)) % 4
    return py, px, (c + 1 - k % 2) % 2


def core_first(k):
    y, z, x, c = place()
    other = k >= 15
    i = jnp.where(other, k - 15, k)
    return (y + far_first(i // 4)) % 4, (x + far_first(i % 4)) % 4, jnp.where(other, 1 - c, c)


def loop(n, body, start=0):
    def step(k, carry):
        body(k)
        return carry

    lax.fori_loop(start, n, step, 0, unroll=UNROLL)


def merge(nums, tops):
    peak = tops[0]
    for top in tops[1:]:
        peak = jnp.maximum(peak, top)
    num, den = 0.0, 0.0
    for part, top in zip(nums, tops):
        w = jnp.exp(top - peak)
        num = num + w * part
        den = den + w
    return num / den, peak + jnp.log(den)


def encode(num, top):
    spot = lax.broadcasted_iota(jnp.int32, (8, 128), 1) % 32
    high = top.astype(BF16).astype(F32)
    middle = (top - high).astype(BF16).astype(F32)
    low = top - high - middle
    terms = jnp.where(spot == 0, high, jnp.where(spot == 1, middle, jnp.where(spot == 2, low, 0.0)))
    return jnp.concatenate([num, terms], axis=0).astype(BF16)


def decode(tiles):
    n = tiles.shape[0]
    a = lax.broadcasted_iota(jnp.int32, (128, 128), 0) // 32
    b = lax.broadcasted_iota(jnp.int32, (128, 128), 1) // 32
    ones = jnp.where(a == b, 1.0, 0.0).astype(BF16)
    sums = jnp.dot(tiles.reshape(16 * n, 128), ones, preferred_element_type=F32)
    values = tiles.astype(F32)
    return [values[i, 0:8] for i in range(n)], [sums[16 * i + 8 : 16 * i + 16] for i in range(n)]


def kernel(
    lengths_ref,
    q_hbm,
    ik_hbm,
    nv_hbm,
    k_hbm,
    v_hbm,
    res_hbm,
    gain_hbm,
    ow_hbm,
    gate_hbm,
    up_hbm,
    att_out,
    upd_out,
    hid_out,
    q_ref,
    ik_ref,
    nv_ref,
    k_ref,
    v_ref,
    res_ref,
    gain_ref,
    ow,
    gate_w,
    up_w,
    gain32,
    s1,
    zd,
    zp,
    zm,
    zrel,
    zfin,
    rsrc,
    rbuf,
    psrc,
    pbuf,
    wbuf,
    z2src,
    z2,
    hsrc,
    hbuf,
    att_v,
    upd_v,
    hid_v,
    local_sems,
    send_sems,
    recv_sems,
    h_sems,
    ready,
):
    y, z, x, c = place()
    t = x * 2 + c
    j = y * 16 + z
    slot_ty = t * 4 + y
    slot_m = y * 8 + t
    barrier = pltpu.get_barrier_semaphore()

    def greet_z(k):
        pl.semaphore_signal(barrier, inc=1, device_id=z_near(k), device_id_type=MESH)

    def greet_plane(k):
        py, px, pc = core_first(k)
        pl.semaphore_signal(
            barrier, inc=1, device_id=(py * 16 + z, px * 2 + pc), device_id_type=MESH
        )

    small = []
    for i, (src, dst) in enumerate(
        (
            (q_hbm, q_ref),
            (k_hbm, k_ref),
            (ik_hbm, ik_ref),
            (v_hbm, v_ref),
            (nv_hbm, nv_ref),
            (res_hbm, res_ref),
            (gain_hbm, gain_ref),
        )
    ):
        small.append(pltpu.make_async_copy(src, dst, local_sems.at[4 + i]))
        if i < 5:
            small[-1].start()
    loop(8, greet_z)
    loop(15, greet_plane)
    partner = (j, x * 2 + 1 - c)
    pl.semaphore_signal(barrier, inc=1, device_id=partner, device_id_type=MESH)
    small[5].start()
    small[6].start()
    ow_load = pltpu.make_async_copy(ow_hbm, ow, local_sems.at[0])
    gate_load = pltpu.make_async_copy(gate_hbm, gate_w, local_sems.at[1])
    up_load = pltpu.make_async_copy(up_hbm, up_w, local_sems.at[2])
    ow_load.start()
    gate_load.start()
    up_load.start()

    for i in range(5):
        small[i].wait()

    scale = 1.0 / math.sqrt(128)
    qs = [q_ref[:, 128 * h : 128 * h + 128].astype(F32) for h in range(16)]
    q_all = jnp.concatenate(qs, axis=0).astype(BF16)
    contract = (((1,), (1,)), ((), ()))
    s_all = lax.dot_general(q_all, k_ref[...], contract, preferred_element_type=F32) * scale
    row = lax.broadcasted_iota(jnp.int32, (8, 512), 0)
    lane = lax.broadcasted_iota(jnp.int32, (8, 512), 1)
    length = jnp.zeros((8, 512), jnp.int32)
    for b in range(8):
        length = jnp.where(row == b, lengths_ref[b], length)
    live = jnp.logical_and(lane // 64 == row, j * 64 + lane % 64 < length)
    ik = ik_ref[...].astype(F32)
    nv = nv_ref[...].astype(F32)
    first = j == 0
    probs, extra, floors, lses = [], [], [], []
    for h in range(16):
        s = s_all[8 * h : 8 * h + 8]
        fresh = jnp.sum(qs[h] * ik, axis=1, keepdims=True) * scale
        fresh = jnp.where(first, fresh, -1e30)
        top = jnp.max(jnp.where(live, s, -10000.0), axis=1, keepdims=True)
        top = jnp.maximum(top, fresh)
        p = jnp.where(live, jnp.exp(s - top), 0.0)
        pnew = jnp.exp(fresh - top)
        floor = jnp.maximum(jnp.sum(p, axis=1, keepdims=True) + pnew, 1.0)
        probs.append(p)
        extra.append(pnew.astype(BF16).astype(F32) * nv)
        floors.append(floor)
        lses.append(top + jnp.log(floor))
    p_all = jnp.concatenate(probs, axis=0).astype(BF16)
    numer = jnp.dot(p_all, v_ref[...], preferred_element_type=F32)
    part = [(numer[8 * h : 8 * h + 8] + extra[h]) / floors[h] for h in range(16)]

    block = lax.broadcasted_iota(jnp.int32, (8, 128), 1) // 32
    for zq in range(4):
        lse_tile = jnp.zeros((8, 128), F32)
        for yy in range(4):
            lse_tile = jnp.where(block == yy, lses[4 * yy + zq], lse_tile)
        for qq in range(4):
            tile = jnp.zeros((8, 128), F32)
            for yy in range(4):
                moved = part[4 * yy + zq]
                shift = (32 * (yy - qq)) % 128
                if shift:
                    moved = pltpu.roll(moved, shift, 1)
                tile = jnp.where(block == yy, moved, tile)
            s1[4 * zq + qq] = encode(tile, lse_tile)

    zd[3] = s1[z]
    zp[4] = s1[(z + 4) % 16]
    zm[3] = s1[(z + 12) % 16]

    pl.semaphore_wait(barrier, 24)
    pl.semaphore_signal(ready, inc=1, device_id=partner, device_id_type=MESH)

    def send_z1(src, dst, step, sem):
        pltpu.make_async_remote_copy(
            src_ref=src,
            dst_ref=dst,
            send_sem=send_sems.at[sem],
            recv_sem=recv_sems.at[sem],
            device_id=(y * 16 + (z + step) % 16, t),
            device_id_type=MESH,
        ).start()

    for d in (4, 3, 2, 1):
        send_z1(s1.at[(z + d + 4) % 16], zp.at[d - 1], d, 0)
        if d < 4:
            send_z1(s1.at[(z + 12 - d) % 16], zm.at[d - 1], 16 - d, 6)
    for d in (3, 2, 1):
        send_z1(s1.at[(z + d) % 16], zd.at[3 + d], d, 7)
        send_z1(s1.at[(z + 16 - d) % 16], zd.at[3 - d], 16 - d, 7)

    ow_load.wait()

    def send_w(k):
        py, px, pc = core_first(k)
        column = pl.multiple_of(512 * (py * 8 + px * 2 + pc), 512)
        pltpu.make_async_remote_copy(
            src_ref=ow.at[:, pl.ds(column, 512)],
            dst_ref=wbuf.at[slot_ty],
            send_sem=send_sems.at[1],
            recv_sem=recv_sems.at[1],
            device_id=(py * 16 + z, px * 2 + pc),
            device_id_type=MESH,
        ).start()

    loop(W_FIRST, send_w)
    own_column = pl.multiple_of(512 * slot_m, 512)
    own_w = pltpu.make_async_copy(
        ow.at[:, pl.ds(own_column, 512)], wbuf.at[slot_ty], local_sems.at[3]
    )
    own_w.start()

    def send_res(k):
        pltpu.make_async_remote_copy(
            src_ref=rsrc,
            dst_ref=rbuf.at[t],
            send_sem=send_sems.at[2],
            recv_sem=recv_sems.at[2],
            device_id=(j, (t + 1 + k) % 8),
            device_id_type=MESH,
        ).start()

    small[5].wait()
    small[6].wait()
    spot = lax.broadcasted_iota(jnp.int32, (32, 128), 1)
    want = lax.broadcasted_iota(jnp.int32, (32, 128), 0) + 32 * (t % 4)
    onehot = jnp.where(spot == want, 1.0, 0.0).astype(BF16)
    rtile = jnp.dot(res_ref[...], onehot, preferred_element_type=F32)
    rsrc[...] = rtile
    rbuf[t] = rtile
    gain32[...] = gain_ref[...].astype(F32).reshape(4, 32, 128)
    pl.semaphore_wait(ready, 1)
    loop(7, send_res)

    def wait(ref, sem):
        pltpu.make_async_copy(ref, ref, sem).wait()

    wait(zp.at[pl.ds(0, 4)], recv_sems.at[0])
    zrel[0] = encode(*merge(*decode(zp[...])))
    send_z1(zrel.at[0], zfin.at[0], 4, 8)
    wait(zm.at[pl.ds(0, 3)], recv_sems.at[6])
    zrel[1] = encode(*merge(*decode(zm[...])))
    send_z1(zrel.at[1], zfin.at[1], 12, 8)
    loop(W_SECOND, send_w, W_FIRST)
    wait(zd.at[pl.ds(0, 6)], recv_sems.at[7])
    num, top = merge(*decode(zd[...]))
    wait(zfin, recv_sems.at[8])
    nums, tops = decode(zfin[...])
    tile = encode(*merge([num] + nums, [top] + tops))
    psrc[...] = tile
    pbuf[slot_ty] = tile

    def send_p(k):
        py, px, pc = plane_peer(k)
        pltpu.make_async_remote_copy(
            src_ref=psrc,
            dst_ref=pbuf.at[slot_ty],
            send_sem=send_sems.at[3],
            recv_sem=recv_sems.at[3],
            device_id=(py * 16 + z, px * 2 + pc),
            device_id_type=MESH,
        ).start()

    loop(31, send_p)
    loop(31, send_w, W_SECOND)
    wait(pbuf.at[pl.ds(0, 31)], recv_sems.at[3])
    nums, tops = decode(pbuf[...])
    atts = [
        merge(nums[4 * i : 4 * i + 4], tops[4 * i : 4 * i + 4])[0] for i in range(8)
    ]
    att = jnp.concatenate(atts, axis=1).astype(BF16)

    wait(wbuf.at[pl.ds(0, 31)], recv_sems.at[1])
    own_w.wait()
    h_part = jnp.dot(att, wbuf[...].reshape(1024, 512), preferred_element_type=F32)
    wait(rbuf.at[pl.ds(0, 7)], recv_sems.at[2])
    here = z // 2 == t
    r_low = jnp.where(here, rbuf[0] + rbuf[1] + rbuf[2] + rbuf[3], 0.0)
    r_high = jnp.where(here, rbuf[4] + rbuf[5] + rbuf[6] + rbuf[7], 0.0)
    r_both = jnp.concatenate([r_low, r_high], axis=1)
    h_even = h_part[:, 0:256] + jnp.where(z % 2 == 0, r_both, 0.0)
    h_odd = h_part[:, 256:512] + jnp.where(z % 2 == 1, r_both, 0.0)
    h_low = jnp.concatenate([h_even, h_odd], axis=0).astype(BF16)
    z2src[...] = h_low
    z2[z] = h_low

    def send_z2(k):
        kv, tp = z_peer(k)
        pltpu.make_async_remote_copy(
            src_ref=z2src,
            dst_ref=z2.at[z],
            send_sem=send_sems.at[4],
            recv_sem=recv_sems.at[4],
            device_id=(kv, tp),
            device_id_type=MESH,
        ).start()

    loop(15, send_z2)

    lane128 = lax.broadcasted_iota(jnp.int32, (128, 32), 0)
    col32 = lax.broadcasted_iota(jnp.int32, (128, 32), 1)
    mine = jnp.zeros((8, 128), F32)
    for tt in range(8):
        mine = jnp.where(t == tt, atts[tt], mine)
    pick = jnp.where(lane128 == col32 + 32 * y, 1.0, 0.0).astype(BF16)
    att_v[...] = jnp.dot(mine.astype(BF16), pick, preferred_element_type=F32).astype(BF16)

    att_save = pltpu.make_async_copy(att_v, att_out, local_sems.at[11])
    att_save.start()

    wait(z2.at[pl.ds(0, 15)], recv_sems.at[4])
    h_sum = jnp.zeros((16, 256), F32)
    for i in range(16):
        h_sum = h_sum + z2[i].astype(F32)
    h_low = h_sum.astype(BF16)
    hsrc[...] = h_low
    hbuf[slot_m] = h_low

    def send_h(k):
        py, px, pc = plane_peer(k)
        pltpu.make_async_remote_copy(
            src_ref=hsrc,
            dst_ref=hbuf.at[slot_m],
            send_sem=send_sems.at[5],
            recv_sem=h_sems.at[k // 8],
            device_id=(py * 16 + z, px * 2 + pc),
            device_id_type=MESH,
        ).start()

    loop(31, send_h)
    gate_load.wait()
    up_load.wait()
    squares = jnp.zeros((8, 128), F32)
    gate = jnp.zeros((8, 52), F32)
    up = jnp.zeros((8, 52), F32)
    for g, step in ((3, 0), (2, 3), (1, 1), (0, 2)):
        from_y = (y + 4 - step) % 4
        wait(hbuf.at[pl.ds(0, 8 if step else 7)], h_sems.at[g])
        gains = gain32[from_y]
        tiles = []
        for m in range(8):
            full = hbuf[8 * from_y + m].astype(F32)
            for i in range(4):
                r, l = 8 * (i // 2), 128 * (i % 2)
                tile = full[r : r + 8, l : l + 128]
                squares = squares + tile * tile
                tiles.append(tile * gains[4 * m + i : 4 * m + i + 1, :])
        part_h = jnp.concatenate(tiles, axis=1).astype(BF16)
        columns = pl.ds(pl.multiple_of(4096 * from_y, 4096), 4096)
        gate = gate + lax.dot_general(
            part_h, gate_w[:, columns], contract, preferred_element_type=F32
        )
        up = up + lax.dot_general(part_h, up_w[:, columns], contract, preferred_element_type=F32)
    source = hbuf[y * 8 + z // 2].astype(F32)
    half = jnp.where(z % 2 == 0, source[0:8], source[8:16])
    tile = jnp.where(t // 4 == 0, half[:, 0:128], half[:, 128:256])
    pick = jnp.where(lane128 == col32 + 32 * (t % 4), 1.0, 0.0).astype(BF16)
    upd_v[...] = jnp.dot(tile.astype(BF16), pick, preferred_element_type=F32).astype(BF16)
    upd_save = pltpu.make_async_copy(upd_v, upd_out, local_sems.at[13])
    upd_save.start()

    mean = jnp.sum(squares, axis=1, keepdims=True) * (1.0 / 16384)
    inverse = lax.rsqrt(mean + norm_eps)
    gate = gate * inverse
    up = up * inverse
    hid_v[...] = (gate / (1.0 + jnp.exp(-gate)) * up).astype(BF16)
    hid_save = pltpu.make_async_copy(hid_v, hid_out, local_sems.at[12])
    hid_save.start()

    wait(zp.at[pl.ds(0, 4)], send_sems.at[0])
    wait(zm.at[pl.ds(0, 3)], send_sems.at[6])
    wait(zd.at[pl.ds(0, 6)], send_sems.at[7])
    wait(zfin, send_sems.at[8])
    wait(wbuf.at[pl.ds(0, 31)], send_sems.at[1])
    wait(rbuf.at[pl.ds(0, 7)], send_sems.at[2])
    wait(pbuf.at[pl.ds(0, 31)], send_sems.at[3])
    wait(z2.at[pl.ds(0, 15)], send_sems.at[4])
    wait(hbuf.at[pl.ds(0, 31)], send_sems.at[5])
    att_save.wait()
    upd_save.wait()
    hid_save.wait()


def save(a, b, c, a_out, b_out, c_out, sems):
    copies = [
        pltpu.make_async_copy(src, dst, sems.at[i])
        for i, (src, dst) in enumerate(((a, a_out), (b, b_out), (c, c_out)))
    ]
    for copy in copies:
        copy.start()
    for copy in copies:
        copy.wait()


def body(
    queries,
    incoming_keys,
    new_values,
    key_cache,
    value_cache,
    lengths,
    residual,
    norm_gain,
    o_weight,
    gate_weight,
    up_weight,
):
    hbm = pl.BlockSpec(memory_space=pltpu.HBM)
    attended, updated, hidden = pl.pallas_call(
        kernel,
        out_shape=(
            jax.ShapeDtypeStruct((8, 32), BF16),
            jax.ShapeDtypeStruct((8, 32), BF16),
            jax.ShapeDtypeStruct((8, 52), BF16),
        ),
        in_specs=[pl.BlockSpec(memory_space=pltpu.SMEM)] + [hbm] * 10,
        out_specs=(hbm, hbm, hbm),
        scratch_shapes=[
            pltpu.VMEM((8, 2048), BF16),
            pltpu.VMEM((8, 128), BF16),
            pltpu.VMEM((8, 128), BF16),
            pltpu.VMEM((512, 128), BF16),
            pltpu.VMEM((512, 128), BF16),
            pltpu.VMEM((8, 32), BF16),
            pltpu.VMEM((128, 128), BF16),
            pltpu.VMEM((32, 16384), BF16),
            pltpu.VMEM((52, 16384), BF16),
            pltpu.VMEM((52, 16384), BF16),
            pltpu.VMEM((4, 32, 128), F32),
            pltpu.VMEM((16, 16, 128), BF16),
            pltpu.VMEM((7, 16, 128), BF16),
            pltpu.VMEM((5, 16, 128), BF16),
            pltpu.VMEM((4, 16, 128), BF16),
            pltpu.VMEM((2, 16, 128), BF16),
            pltpu.VMEM((2, 16, 128), BF16),
            pltpu.VMEM((8, 128), F32),
            pltpu.VMEM((8, 8, 128), F32),
            pltpu.VMEM((16, 128), BF16),
            pltpu.VMEM((32, 16, 128), BF16),
            pltpu.VMEM((32, 32, 512), BF16),
            pltpu.VMEM((16, 256), BF16),
            pltpu.VMEM((16, 16, 256), BF16),
            pltpu.VMEM((16, 256), BF16),
            pltpu.VMEM((32, 16, 256), BF16),
            pltpu.VMEM((8, 32), BF16),
            pltpu.VMEM((8, 32), BF16),
            pltpu.VMEM((8, 52), BF16),
            pltpu.SemaphoreType.DMA((14,)),
            pltpu.SemaphoreType.DMA((9,)),
            pltpu.SemaphoreType.DMA((9,)),
            pltpu.SemaphoreType.DMA((4,)),
            pltpu.SemaphoreType.REGULAR,
        ],
        compiler_params=pltpu.CompilerParams(
            collective_id=0, has_side_effects=True, vmem_limit_bytes=63 * 1024 * 1024
        ),
        name="decode_layer",
    )(
        lengths,
        queries,
        incoming_keys,
        new_values,
        key_cache.reshape(512, 128),
        value_cache.reshape(512, 128),
        residual,
        norm_gain.reshape(128, 128),
        o_weight.reshape(32, 16384),
        gate_weight,
        up_weight,
    )
    attended, updated, hidden = pl.pallas_call(
        save,
        out_shape=tuple(jax.ShapeDtypeStruct(a.shape, a.dtype) for a in (attended, updated, hidden)),
        in_specs=[hbm] * 3,
        out_specs=(hbm, hbm, hbm),
        scratch_shapes=[pltpu.SemaphoreType.DMA((3,))],
        compiler_params=pltpu.CompilerParams(vmem_limit_bytes=63 * 1024 * 1024),
        name="save_results",
    )(attended, updated, hidden)
    return attended.reshape(8, 1, 32), updated, hidden


def solution(mesh):
    in_specs = (
        P(None, "tp"),
        P(None, "tp"),
        P(None, "tp"),
        P(None, "kvseq", "tp", None),
        P(None, "kvseq", "tp", None),
        P(),
        P(None, ("kvseq", "tp")),
        P(),
        P("tp", "kvseq", None),
        P(("kvseq", "tp"), None),
        P(("kvseq", "tp"), None),
    )
    out_specs = (P(None, "tp", "kvseq"), P(None, ("kvseq", "tp")), P(None, ("kvseq", "tp")))
    return jax.shard_map(body, mesh=mesh, in_specs=in_specs, out_specs=out_specs, check_vma=False)
```

```python
import math

import jax
import jax.numpy as jnp
from jax import lax
from jax.experimental import pallas as pl
from jax.experimental.pallas import tpu as pltpu
from jax.sharding import PartitionSpec as P

norm_eps = 1e-05
MESH = pl.DeviceIdType.MESH
F32, BF16 = jnp.float32, jnp.bfloat16
UNROLL = True
W_FIRST, W_SECOND = 12, 22


def place():
    kv, tp = lax.axis_index("kvseq"), lax.axis_index("tp")
    return kv // 16, kv % 16, tp // 2, tp % 2


def z_peer(k):
    y, z, x, c = place()
    step = jnp.where(k % 2 == 0, 8 + k // 2, 8 - (k + 1) // 2)
    return (y * 16 + (z + step) % 16, x * 2 + c)


def z_near(k):
    y, z, x, c = place()
    step = jnp.where(k % 2 == 0, 4 - k // 2, 12 + k // 2)
    return (y * 16 + (z + step) % 16, x * 2 + c)


def far_first(a):
    return jnp.where(a == 0, 2, jnp.where(a == 1, 1, jnp.where(a == 2, 3, 0)))


def plane_peer(k):
    y, z, x, c = place()
    py = (y + far_first(k // 8)) % 4
    px = (x + far_first((k // 2) % 4)) % 4
    return py, px, (c + 1 - k % 2) % 2


def core_first(k):
    y, z, x, c = place()
    other = k >= 15
    i = jnp.where(other, k - 15, k)
    return (y + far_first(i // 4)) % 4, (x + far_first(i % 4)) % 4, jnp.where(other, 1 - c, c)


def loop(n, body, start=0):
    def step(k, carry):
        body(k)
        return carry

    lax.fori_loop(start, n, step, 0, unroll=UNROLL)


def merge(nums, tops):
    peak = tops[0]
    for top in tops[1:]:
        peak = jnp.maximum(peak, top)
    num, den = 0.0, 0.0
    for part, top in zip(nums, tops):
        w = jnp.exp(top - peak)
        num = num + w * part
        den = den + w
    return num / den, peak + jnp.log(den)


def encode(num, top):
    spot = lax.broadcasted_iota(jnp.int32, (8, 128), 1) % 32
    high = top.astype(BF16).astype(F32)
    middle = (top - high).astype(BF16).astype(F32)
    low = top - high - middle
    terms = jnp.where(spot == 0, high, jnp.where(spot == 1, middle, jnp.where(spot == 2, low, 0.0)))
    return jnp.concatenate([num, terms], axis=0).astype(BF16)


def decode(tiles):
    n = tiles.shape[0]
    a = lax.broadcasted_iota(jnp.int32, (128, 128), 0) // 32
    b = lax.broadcasted_iota(jnp.int32, (128, 128), 1) // 32
    ones = jnp.where(a == b, 1.0, 0.0).astype(BF16)
    sums = jnp.dot(tiles.reshape(16 * n, 128), ones, preferred_element_type=F32)
    values = tiles.astype(F32)
    return [values[i, 0:8] for i in range(n)], [sums[16 * i + 8 : 16 * i + 16] for i in range(n)]


def kernel(
    lengths_ref,
    q_hbm,
    ik_hbm,
    nv_hbm,
    k_hbm,
    v_hbm,
    res_hbm,
    gain_hbm,
    ow_hbm,
    gate_hbm,
    up_hbm,
    att_out,
    upd_out,
    hid_out,
    q_ref,
    ik_ref,
    nv_ref,
    k_ref,
    v_ref,
    res_ref,
    gain_ref,
    ow,
    gate_w,
    up_w,
    gain32,
    s1,
    zd,
    zp,
    zm,
    zrel,
    zfin,
    rsrc,
    rbuf,
    psrc,
    pbuf,
    wbuf,
    z2src,
    z2,
    hsrc,
    hbuf,
    att_v,
    upd_v,
    hid_v,
    local_sems,
    send_sems,
    recv_sems,
    h_sems,
    ready,
):
    y, z, x, c = place()
    t = x * 2 + c
    j = y * 16 + z
    slot_ty = t * 4 + y
    slot_m = y * 8 + t
    barrier = pltpu.get_barrier_semaphore()

    def greet_z(k):
        pl.semaphore_signal(barrier, inc=1, device_id=z_near(k), device_id_type=MESH)

    def greet_plane(k):
        py, px, pc = core_first(k)
        pl.semaphore_signal(
            barrier, inc=1, device_id=(py * 16 + z, px * 2 + pc), device_id_type=MESH
        )

    small = []
    for i, (src, dst) in enumerate(
        (
            (q_hbm, q_ref),
            (k_hbm, k_ref),
            (ik_hbm, ik_ref),
            (v_hbm, v_ref),
            (nv_hbm, nv_ref),
            (res_hbm, res_ref),
            (gain_hbm, gain_ref),
        )
    ):
        small.append(pltpu.make_async_copy(src, dst, local_sems.at[4 + i]))
        if i < 5:
            small[-1].start()
    loop(8, greet_z)
    loop(15, greet_plane)
    partner = (j, x * 2 + 1 - c)
    pl.semaphore_signal(barrier, inc=1, device_id=partner, device_id_type=MESH)
    small[5].start()
    small[6].start()
    ow_load = pltpu.make_async_copy(ow_hbm, ow, local_sems.at[0])
    gate_load = pltpu.make_async_copy(gate_hbm, gate_w, local_sems.at[1])
    up_load = pltpu.make_async_copy(up_hbm, up_w, local_sems.at[2])
    ow_load.start()
    gate_load.start()
    up_load.start()

    for i in range(5):
        small[i].wait()

    scale = 1.0 / math.sqrt(128)
    qs = [q_ref[:, 128 * h : 128 * h + 128].astype(F32) for h in range(16)]
    q_all = jnp.concatenate(qs, axis=0).astype(BF16)
    contract = (((1,), (1,)), ((), ()))
    s_all = lax.dot_general(q_all, k_ref[...], contract, preferred_element_type=F32) * scale
    row = lax.broadcasted_iota(jnp.int32, (8, 512), 0)
    lane = lax.broadcasted_iota(jnp.int32, (8, 512), 1)
    length = jnp.zeros((8, 512), jnp.int32)
    for b in range(8):
        length = jnp.where(row == b, lengths_ref[b], length)
    live = jnp.logical_and(lane // 64 == row, j * 64 + lane % 64 < length)
    ik = ik_ref[...].astype(F32)
    nv = nv_ref[...].astype(F32)
    first = j == 0
    probs, extra, floors, lses = [], [], [], []
    for h in range(16):
        s = s_all[8 * h : 8 * h + 8]
        fresh = jnp.sum(qs[h] * ik, axis=1, keepdims=True) * scale
        fresh = jnp.where(first, fresh, -1e30)
        top = jnp.max(jnp.where(live, s, -10000.0), axis=1, keepdims=True)
        top = jnp.maximum(top, fresh)
        p = jnp.where(live, jnp.exp(s - top), 0.0)
        pnew = jnp.exp(fresh - top)
        floor = jnp.maximum(jnp.sum(p, axis=1, keepdims=True) + pnew, 1.0)
        probs.append(p)
        extra.append(pnew.astype(BF16).astype(F32) * nv)
        floors.append(floor)
        lses.append(top + jnp.log(floor))
    p_all = jnp.concatenate(probs, axis=0).astype(BF16)
    numer = jnp.dot(p_all, v_ref[...], preferred_element_type=F32)
    part = [(numer[8 * h : 8 * h + 8] + extra[h]) / floors[h] for h in range(16)]

    block = lax.broadcasted_iota(jnp.int32, (8, 128), 1) // 32
    for zq in range(4):
        lse_tile = jnp.zeros((8, 128), F32)
        for yy in range(4):
            lse_tile = jnp.where(block == yy, lses[4 * yy + zq], lse_tile)
        for qq in range(4):
            tile = jnp.zeros((8, 128), F32)
            for yy in range(4):
                moved = part[4 * yy + zq]
                shift = (32 * (yy - qq)) % 128
                if shift:
                    moved = pltpu.roll(moved, shift, 1)
                tile = jnp.where(block == yy, moved, tile)
            s1[4 * zq + qq] = encode(tile, lse_tile)

    small[5].wait()
    small[6].wait()
    spot = lax.broadcasted_iota(jnp.int32, (32, 128), 1)
    want = lax.broadcasted_iota(jnp.int32, (32, 128), 0) + 32 * (t % 4)
    onehot = jnp.where(spot == want, 1.0, 0.0).astype(BF16)
    rtile = jnp.dot(res_ref[...], onehot, preferred_element_type=F32)
    rsrc[...] = rtile
    rbuf[t] = rtile
    gain32[...] = gain_ref[...].astype(F32).reshape(4, 32, 128)
    zd[3] = s1[z]
    zp[4] = s1[(z + 4) % 16]
    zm[3] = s1[(z + 12) % 16]

    pl.semaphore_wait(barrier, 24)
    pl.semaphore_signal(ready, inc=1, device_id=partner, device_id_type=MESH)

    def send_z1(src, dst, step, sem):
        pltpu.make_async_remote_copy(
            src_ref=src,
            dst_ref=dst,
            send_sem=send_sems.at[sem],
            recv_sem=recv_sems.at[sem],
            device_id=(y * 16 + (z + step) % 16, t),
            device_id_type=MESH,
        ).start()

    for d in (4, 3, 2, 1):
        send_z1(s1.at[(z + d + 4) % 16], zp.at[d - 1], d, 0)
        if d < 4:
            send_z1(s1.at[(z + 12 - d) % 16], zm.at[d - 1], 16 - d, 6)
    for d in (3, 2, 1):
        send_z1(s1.at[(z + d) % 16], zd.at[3 + d], d, 7)
        send_z1(s1.at[(z + 16 - d) % 16], zd.at[3 - d], 16 - d, 7)

    ow_load.wait()

    def send_w(k):
        py, px, pc = core_first(k)
        column = pl.multiple_of(512 * (py * 8 + px * 2 + pc), 512)
        pltpu.make_async_remote_copy(
            src_ref=ow.at[:, pl.ds(column, 512)],
            dst_ref=wbuf.at[slot_ty],
            send_sem=send_sems.at[1],
            recv_sem=recv_sems.at[1],
            device_id=(py * 16 + z, px * 2 + pc),
            device_id_type=MESH,
        ).start()

    loop(W_FIRST, send_w)
    own_column = pl.multiple_of(512 * slot_m, 512)
    own_w = pltpu.make_async_copy(
        ow.at[:, pl.ds(own_column, 512)], wbuf.at[slot_ty], local_sems.at[3]
    )
    own_w.start()

    def send_res(k):
        pltpu.make_async_remote_copy(
            src_ref=rsrc,
            dst_ref=rbuf.at[t],
            send_sem=send_sems.at[2],
            recv_sem=recv_sems.at[2],
            device_id=(j, (t + 1 + k) % 8),
            device_id_type=MESH,
        ).start()

    pl.semaphore_wait(ready, 1)
    loop(7, send_res)

    def wait(ref, sem):
        pltpu.make_async_copy(ref, ref, sem).wait()

    wait(zp.at[pl.ds(0, 4)], recv_sems.at[0])
    zrel[0] = encode(*merge(*decode(zp[...])))
    send_z1(zrel.at[0], zfin.at[0], 4, 8)
    wait(zm.at[pl.ds(0, 3)], recv_sems.at[6])
    zrel[1] = encode(*merge(*decode(zm[...])))
    send_z1(zrel.at[1], zfin.at[1], 12, 8)
    loop(W_SECOND, send_w, W_FIRST)
    wait(zd.at[pl.ds(0, 6)], recv_sems.at[7])
    num, top = merge(*decode(zd[...]))
    wait(zfin, recv_sems.at[8])
    nums, tops = decode(zfin[...])
    tile = encode(*merge([num] + nums, [top] + tops))
    psrc[...] = tile
    pbuf[slot_ty] = tile

    def send_p(k):
        py, px, pc = plane_peer(k)
        pltpu.make_async_remote_copy(
            src_ref=psrc,
            dst_ref=pbuf.at[slot_ty],
            send_sem=send_sems.at[3],
            recv_sem=recv_sems.at[3],
            device_id=(py * 16 + z, px * 2 + pc),
            device_id_type=MESH,
        ).start()

    loop(31, send_p)
    loop(31, send_w, W_SECOND)
    wait(pbuf.at[pl.ds(0, 31)], recv_sems.at[3])
    nums, tops = decode(pbuf[...])
    atts = [
        merge(nums[4 * i : 4 * i + 4], tops[4 * i : 4 * i + 4])[0] for i in range(8)
    ]
    att = jnp.concatenate(atts, axis=1).astype(BF16)

    wait(wbuf.at[pl.ds(0, 31)], recv_sems.at[1])
    own_w.wait()
    h_part = jnp.dot(att, wbuf[...].reshape(1024, 512), preferred_element_type=F32)
    wait(rbuf.at[pl.ds(0, 7)], recv_sems.at[2])
    here = z // 2 == t
    r_low = jnp.where(here, rbuf[0] + rbuf[1] + rbuf[2] + rbuf[3], 0.0)
    r_high = jnp.where(here, rbuf[4] + rbuf[5] + rbuf[6] + rbuf[7], 0.0)
    r_both = jnp.concatenate([r_low, r_high], axis=1)
    h_even = h_part[:, 0:256] + jnp.where(z % 2 == 0, r_both, 0.0)
    h_odd = h_part[:, 256:512] + jnp.where(z % 2 == 1, r_both, 0.0)
    h_low = jnp.concatenate([h_even, h_odd], axis=0).astype(BF16)
    z2src[...] = h_low
    z2[z] = h_low

    def send_z2(k):
        kv, tp = z_peer(k)
        pltpu.make_async_remote_copy(
            src_ref=z2src,
            dst_ref=z2.at[z],
            send_sem=send_sems.at[4],
            recv_sem=recv_sems.at[4],
            device_id=(kv, tp),
            device_id_type=MESH,
        ).start()

    loop(15, send_z2)

    lane128 = lax.broadcasted_iota(jnp.int32, (128, 32), 0)
    col32 = lax.broadcasted_iota(jnp.int32, (128, 32), 1)
    mine = jnp.zeros((8, 128), F32)
    for tt in range(8):
        mine = jnp.where(t == tt, atts[tt], mine)
    pick = jnp.where(lane128 == col32 + 32 * y, 1.0, 0.0).astype(BF16)
    att_v[...] = jnp.dot(mine.astype(BF16), pick, preferred_element_type=F32).astype(BF16)

    att_save = pltpu.make_async_copy(att_v, att_out, local_sems.at[11])
    att_save.start()

    wait(z2.at[pl.ds(0, 15)], recv_sems.at[4])
    h_sum = jnp.zeros((16, 256), F32)
    for i in range(16):
        h_sum = h_sum + z2[i].astype(F32)
    h_low = h_sum.astype(BF16)
    hsrc[...] = h_low
    hbuf[slot_m] = h_low

    def send_h(k):
        py, px, pc = plane_peer(k)
        pltpu.make_async_remote_copy(
            src_ref=hsrc,
            dst_ref=hbuf.at[slot_m],
            send_sem=send_sems.at[5],
            recv_sem=h_sems.at[k // 8],
            device_id=(py * 16 + z, px * 2 + pc),
            device_id_type=MESH,
        ).start()

    loop(31, send_h)
    gate_load.wait()
    up_load.wait()
    squares = jnp.zeros((8, 128), F32)
    gate = jnp.zeros((8, 52), F32)
    up = jnp.zeros((8, 52), F32)
    for g, step in ((3, 0), (2, 3), (1, 1), (0, 2)):
        from_y = (y + 4 - step) % 4
        wait(hbuf.at[pl.ds(0, 8 if step else 7)], h_sems.at[g])
        if step == 0:
            source = hbuf[y * 8 + z // 2].astype(F32)
            half = jnp.where(z % 2 == 0, source[0:8], source[8:16])
            tile = jnp.where(t // 4 == 0, half[:, 0:128], half[:, 128:256])
            pick = jnp.where(lane128 == col32 + 32 * (t % 4), 1.0, 0.0).astype(BF16)
            upd_v[...] = jnp.dot(tile.astype(BF16), pick, preferred_element_type=F32).astype(BF16)
            upd_save = pltpu.make_async_copy(upd_v, upd_out, local_sems.at[13])
            upd_save.start()
        gains = gain32[from_y]
        tiles = []
        for m in range(8):
            full = hbuf[8 * from_y + m].astype(F32)
            for i in range(4):
                r, l = 8 * (i // 2), 128 * (i % 2)
                tile = full[r : r + 8, l : l + 128]
                squares = squares + tile * tile
                tiles.append(tile * gains[4 * m + i : 4 * m + i + 1, :])
        part_h = jnp.concatenate(tiles, axis=1).astype(BF16)
        columns = pl.ds(pl.multiple_of(4096 * from_y, 4096), 4096)
        gate = gate + lax.dot_general(
            part_h, gate_w[:, columns], contract, preferred_element_type=F32
        )
        up = up + lax.dot_general(part_h, up_w[:, columns], contract, preferred_element_type=F32)
    mean = jnp.sum(squares, axis=1, keepdims=True) * (1.0 / 16384)
    inverse = lax.rsqrt(mean + norm_eps)
    gate = gate * inverse
    up = up * inverse
    hid_v[...] = (gate / (1.0 + jnp.exp(-gate)) * up).astype(BF16)
    hid_save = pltpu.make_async_copy(hid_v, hid_out, local_sems.at[12])
    hid_save.start()

    wait(zp.at[pl.ds(0, 4)], send_sems.at[0])
    wait(zm.at[pl.ds(0, 3)], send_sems.at[6])
    wait(zd.at[pl.ds(0, 6)], send_sems.at[7])
    wait(zfin, send_sems.at[8])
    wait(wbuf.at[pl.ds(0, 31)], send_sems.at[1])
    wait(rbuf.at[pl.ds(0, 7)], send_sems.at[2])
    wait(pbuf.at[pl.ds(0, 31)], send_sems.at[3])
    wait(z2.at[pl.ds(0, 15)], send_sems.at[4])
    wait(hbuf.at[pl.ds(0, 31)], send_sems.at[5])
    att_save.wait()
    upd_save.wait()
    hid_save.wait()


def save(a, b, c, a_out, b_out, c_out, sems):
    copies = [
        pltpu.make_async_copy(src, dst, sems.at[i])
        for i, (src, dst) in enumerate(((a, a_out), (b, b_out), (c, c_out)))
    ]
    for copy in copies:
        copy.start()
    for copy in copies:
        copy.wait()


def body(
    queries,
    incoming_keys,
    new_values,
    key_cache,
    value_cache,
    lengths,
    residual,
    norm_gain,
    o_weight,
    gate_weight,
    up_weight,
):
    hbm = pl.BlockSpec(memory_space=pltpu.HBM)
    attended, updated, hidden = pl.pallas_call(
        kernel,
        out_shape=(
            jax.ShapeDtypeStruct((8, 32), BF16),
            jax.ShapeDtypeStruct((8, 32), BF16),
            jax.ShapeDtypeStruct((8, 52), BF16),
        ),
        in_specs=[pl.BlockSpec(memory_space=pltpu.SMEM)] + [hbm] * 10,
        out_specs=(hbm, hbm, hbm),
        scratch_shapes=[
            pltpu.VMEM((8, 2048), BF16),
            pltpu.VMEM((8, 128), BF16),
            pltpu.VMEM((8, 128), BF16),
            pltpu.VMEM((512, 128), BF16),
            pltpu.VMEM((512, 128), BF16),
            pltpu.VMEM((8, 32), BF16),
            pltpu.VMEM((128, 128), BF16),
            pltpu.VMEM((32, 16384), BF16),
            pltpu.VMEM((52, 16384), BF16),
            pltpu.VMEM((52, 16384), BF16),
            pltpu.VMEM((4, 32, 128), F32),
            pltpu.VMEM((16, 16, 128), BF16),
            pltpu.VMEM((7, 16, 128), BF16),
            pltpu.VMEM((5, 16, 128), BF16),
            pltpu.VMEM((4, 16, 128), BF16),
            pltpu.VMEM((2, 16, 128), BF16),
            pltpu.VMEM((2, 16, 128), BF16),
            pltpu.VMEM((8, 128), F32),
            pltpu.VMEM((8, 8, 128), F32),
            pltpu.VMEM((16, 128), BF16),
            pltpu.VMEM((32, 16, 128), BF16),
            pltpu.VMEM((32, 32, 512), BF16),
            pltpu.VMEM((16, 256), BF16),
            pltpu.VMEM((16, 16, 256), BF16),
            pltpu.VMEM((16, 256), BF16),
            pltpu.VMEM((32, 16, 256), BF16),
            pltpu.VMEM((8, 32), BF16),
            pltpu.VMEM((8, 32), BF16),
            pltpu.VMEM((8, 52), BF16),
            pltpu.SemaphoreType.DMA((14,)),
            pltpu.SemaphoreType.DMA((9,)),
            pltpu.SemaphoreType.DMA((9,)),
            pltpu.SemaphoreType.DMA((4,)),
            pltpu.SemaphoreType.REGULAR,
        ],
        compiler_params=pltpu.CompilerParams(
            collective_id=0, has_side_effects=True, vmem_limit_bytes=63 * 1024 * 1024
        ),
        name="decode_layer",
    )(
        lengths,
        queries,
        incoming_keys,
        new_values,
        key_cache.reshape(512, 128),
        value_cache.reshape(512, 128),
        residual,
        norm_gain.reshape(128, 128),
        o_weight.reshape(32, 16384),
        gate_weight,
        up_weight,
    )
    attended, updated, hidden = pl.pallas_call(
        save,
        out_shape=tuple(jax.ShapeDtypeStruct(a.shape, a.dtype) for a in (attended, updated, hidden)),
        in_specs=[hbm] * 3,
        out_specs=(hbm, hbm, hbm),
        scratch_shapes=[pltpu.SemaphoreType.DMA((3,))],
        compiler_params=pltpu.CompilerParams(vmem_limit_bytes=63 * 1024 * 1024),
        name="save_results",
    )(attended, updated, hidden)
    return attended.reshape(8, 1, 32), updated, hidden


def solution(mesh):
    in_specs = (
        P(None, "tp"),
        P(None, "tp"),
        P(None, "tp"),
        P(None, "kvseq", "tp", None),
        P(None, "kvseq", "tp", None),
        P(),
        P(None, ("kvseq", "tp")),
        P(),
        P("tp", "kvseq", None),
        P(("kvseq", "tp"), None),
        P(("kvseq", "tp"), None),
    )
    out_specs = (P(None, "tp", "kvseq"), P(None, ("kvseq", "tp")), P(None, ("kvseq", "tp")))
    return jax.shard_map(body, mesh=mesh, in_specs=in_specs, out_specs=out_specs, check_vma=False)
```
